128 devices in a mesh: row: 16 (over x, y), col: 8 (over z, core).
Axes of the slice: x: 4, y: 4, z: 4, core: 2. Of those that a mesh axis runs over, the one named last changes fastest.
Arguments:
- tokens: bfloat16 [2048, 4096], P('row', 'col'), may hold values from -6 to 6
- weight_in: bfloat16 [4096, 8192], P('row', 'col'), may hold values from -0.09375 to 0.09375
- weight_out: bfloat16 [8192, 4096], P('row', 'col'), may hold values from -0.0625 to 0.0625
- cotangent: bfloat16 [2048, 4096], P('row', 'col'), may hold values from -3 to 3
Outputs:
- output: bfloat16 [2048, 4096], P('row', 'col')
- grad_tokens: bfloat16 [2048, 4096], P('row', 'col')
- grad_weight_in: bfloat16 [4096, 8192], P('row', 'col')
- grad_weight_out: bfloat16 [8192, 4096], P('row', 'col')
The draws below stay inside these ranges and needn't reach their ends.
All inputs are finite; a program needn't handle non-finite values.
Results may differ from the reference program's by a relative error of at most 0.005.
Values may be sent and summed in bfloat16 or wider, within the bound.
A program may use at most 128 MiB of HBM per device.

```python
import math
import jax
import jax.numpy as jnp

D = 4096
FF = 8192
TOKENS = 2048


def shard_levels(own_key, dims, cuts, least, largest):
    def one(axis_at, parts):
        draws = jax.random.uniform(jax.random.fold_in(jax.random.fold_in(own_key, 6), axis_at), (parts,), jnp.float32, least / len(cuts), largest / len(cuts))
        return jnp.repeat(jnp.exp(draws), dims[axis_at] // parts).reshape((-1,) + (1,) * (len(dims) - axis_at - 1))

    factor_of = one(*cuts[0])
    for cut in cuts[1:]:
        factor_of = factor_of * one(*cut)
    return factor_of


def normal_values(stream_key, shape, spread, bound, split=(), dtype=jnp.bfloat16):
    result = spread * jax.random.normal(stream_key, shape, jnp.float32)
    if split:
        result = result * shard_levels(stream_key, shape, split, -0.22, 0.18)
    return jnp.clip(result, -bound, bound).astype(dtype)


def setup_inputs(seed: int = 0) -> dict:
    streams_of = jax.random.split(jax.random.key(seed), 5)
    return {
        "tokens": normal_values(streams_of[0], (TOKENS, D), 1.0, 6.0, ((0, 16), (1, 8))),
        "weight_in": normal_values(streams_of[1], (D, FF), D ** -0.5, 0.09375, ((0, 16), (1, 8))),
        "weight_out": normal_values(streams_of[2], (FF, D), FF ** -0.5, 0.0625, ((0, 16), (1, 8))),
        "cotangent": normal_values(streams_of[3], (TOKENS, D), 0.5, 3.0, ((0, 16), (1, 8))),
    }


gelu_scale = math.sqrt(2.0 / math.pi)
cubic_term = 0.044715

def activate(preact):
    argument = gelu_scale * (preact + cubic_term * preact * preact * preact)
    return 0.5 * preact * (1.0 + jnp.tanh(argument))

def activate_slope(preact):
    argument = gelu_scale * (preact + cubic_term * preact * preact * preact)
    tanh_value = jnp.tanh(argument)
    return 0.5 * (1.0 + tanh_value) + 0.5 * preact * (1.0 - tanh_value * tanh_value) * gelu_scale * (1.0 + 3.0 * cubic_term * preact * preact)

def reference(tokens, weight_in, weight_out, cotangent):
    preact = jnp.dot(tokens, weight_in, preferred_element_type=jnp.float32)
    hidden = activate(preact).astype(jnp.bfloat16)
    output = jnp.dot(hidden, weight_out, preferred_element_type=jnp.float32).astype(jnp.bfloat16)
    grad_hidden = jnp.dot(cotangent, weight_out.T, preferred_element_type=jnp.float32)
    grad_preact = (grad_hidden * activate_slope(preact)).astype(jnp.bfloat16)
    grad_tokens = jnp.dot(grad_preact, weight_in.T, preferred_element_type=jnp.float32).astype(jnp.bfloat16)
    grad_weight_in = jnp.dot(tokens.T, grad_preact, preferred_element_type=jnp.float32).astype(jnp.bfloat16)
    grad_weight_out = jnp.dot(hidden.T, cotangent, preferred_element_type=jnp.float32).astype(jnp.bfloat16)
    return (output, grad_tokens, grad_weight_in, grad_weight_out)
```

```python
import functools
import math

import jax
import jax.numpy as jnp
from jax import lax
from jax.experimental import pallas as pl
from jax.experimental.pallas import tpu as pltpu
from jax.sharding import PartitionSpec as P

MESH = pl.DeviceIdType.MESH
BF16 = jnp.bfloat16
F32 = jnp.float32

gelu_scale = math.sqrt(2.0 / math.pi)
cubic_term = 0.044715

chunks = 8
m = 128 // chunks
n = 16 * m
tz = n // 8
W = 512
pieces = 4

relay_gather_1, relay_gather_2 = False, False
relay_sum_z, relay_gather_z = False, False
relay_sum_1, relay_sum_2 = False, False


def activate_both(preact):
    square = preact * preact
    tanh_value = jnp.tanh(gelu_scale * (preact + cubic_term * square * preact))
    half = 0.5 * (1.0 + tanh_value)
    slope = half + 0.5 * preact * (1.0 - tanh_value * tanh_value) * gelu_scale * (
        1.0 + 3.0 * cubic_term * square
    )
    return preact * half, slope


def dot_nn(left, right):
    return jnp.dot(left, right, preferred_element_type=F32)


def dot_nt(left, right):
    return lax.dot_general(
        left, right, (((1,), (1,)), ((), ())), preferred_element_type=F32
    )


def dot_tn(left, right):
    return lax.dot_general(
        left, right, (((0,), (0,)), ((), ())), preferred_element_type=F32
    )


def kernel(
    x_ref, c_ref, win_ref, w2_ref,
    out_ref, gx_ref, gw1_ref, gw2_ref,
    ax, ac, part, ks, kr, zs, zt, zr, hg, os, gs, t1, r1, u, t2, r2, acc,
    w1, gw1, stay, back,
    s_g, r_g, s_k, r_k, s_z, r_z, s_h, r_h, s_p, r_p, s_o, r_o, s_w, r_w,
):
    row, col = lax.axis_index("row"), lax.axis_index("col")
    x, y, z, k = row // 4, lax.rem(row, 4), col // 2, lax.rem(col, 2)
    sign = 1 - 2 * k

    def at(base, step):
        return lax.rem(base + step * sign + 4, 4)

    def on_x(p):
        return (p * 4 + y, col)

    def on_y(p):
        return (x * 4 + p, col)

    def on_z(p):
        return (row, p * 2 + k)

    partner = (row, z * 2 + 1 - k)

    def copy(src, dst, send, recv, device):
        return pltpu.make_async_remote_copy(
            src_ref=src, dst_ref=dst, send_sem=send, recv_sem=recv,
            device_id=device, device_id_type=MESH,
        )

    def shift(b):
        return lax.rem(b + x + y, 4)

    def turn_target(b):
        return (lax.rem(z - shift(b) + 4, 4) * 4 + b, x * 2 + y // 2)

    def turn_source(slot):
        return (z * 4 + 2 * k + slot, lax.rem(x + y + z + 2 * k + slot, 4) * 2 + y // 2)

    home = (x == z) & (lax.rem(x + 2 * y, 4) == 0) & (k == y // 2)

    def is_home(j):
        return home & (lax.rem(y, 2) == j)

    barrier = pltpu.get_barrier_semaphore()

    def greet(device):
        pl.semaphore_signal(barrier, inc=1, device_id=device, device_id_type=MESH)

    for j in (1, 2, 3):
        greet(on_x(lax.rem(x + j, 4)))
        greet(on_y(lax.rem(y + j, 4)))
        greet(on_z(lax.rem(z + j, 4)))
    greet(partner)
    for j in (0, 1):

        @pl.when(jnp.logical_not(is_home(j)))
        def _():
            greet(turn_target(2 * k + j))
            greet(turn_source(j))

    def load(i, _):
        ax[i, x, y] = x_ref[pl.ds(pl.multiple_of(i * m, m), m), :]
        ac[i, x, y] = c_ref[pl.ds(pl.multiple_of(i * m, m), m), :]
        return 0

    lax.fori_loop(0, chunks, load, 0)
    acc[...] = jnp.zeros_like(acc)
    pl.semaphore_wait(barrier, 14 - 2 * home.astype(jnp.int32))

    size = 256 // pieces

    class Turn:
        def __init__(self, way, source, middle, target):
            self.way, self.source, self.middle, self.target = way, source, middle, target

        def move_1(self, j, q):
            where = (self.way, 0, j, q)
            rows = pl.ds(q * size, size)
            return copy(
                self.source(j, rows), self.middle.at[j, rows], s_w.at[where], r_w.at[where],
                on_z(lax.rem(z + shift(2 * k + j), 4)),
            )

        def move_2(self, j, q, slot):
            send, recv = (self.way, 1, j, q), (self.way, 1, slot, q)
            rows = pl.ds(q * size, size)
            return copy(
                self.middle.at[j, rows], self.target(slot, rows),
                s_w.at[send], r_w.at[recv], turn_target(2 * k + j),
            )

        def stay_1(self, j, q):
            rows = pl.ds(q * size, size)
            return pltpu.make_async_copy(
                self.source(j, rows), self.middle.at[j, rows], r_w.at[self.way, 0, j, q]
            )

        def stay_2(self, j, q):
            rows = pl.ds(q * size, size)
            return pltpu.make_async_copy(
                self.middle.at[j, rows], self.target(j, rows), r_w.at[self.way, 1, j, q]
            )

        def either(self, condition, yes, no):
            pl.when(condition)(yes)
            pl.when(jnp.logical_not(condition))(no)

        def start(self):
            for q in range(pieces):
                for j in (0, 1):
                    self.either(
                        shift(2 * k + j) == 0,
                        lambda: self.stay_1(j, q).start(),
                        lambda: self.move_1(j, q).start(),
                    )

        def forward(self):
            slot = lax.rem(y, 2)
            for q in range(pieces):
                for j in (0, 1):
                    self.move_1(j, q).wait_recv()
                    self.either(
                        is_home(j),
                        lambda: self.stay_2(j, q).start(),
                        lambda: self.move_2(j, q, slot).start(),
                    )

        def wait_recv(self):
            for q in range(pieces):
                for slot in (0, 1):
                    self.move_2(0, q, slot).wait_recv()

        def wait_send(self):
            for q in range(pieces):
                for j in (0, 1):
                    pl.when(shift(2 * k + j) != 0)(lambda: self.move_1(j, q).wait_send())
                    pl.when(jnp.logical_not(is_home(j)))(
                        lambda: self.move_2(j, q, 0).wait_send()
                    )

    def half(slot):
        return pl.ds(pl.multiple_of(slot * W, W), W)

    turn_in = Turn(
        0, lambda j, rows: win_ref.at[rows, half(j)], stay, lambda slot, rows: w1.at[slot, rows]
    )
    turn_out = Turn(
        1, lambda j, rows: gw1.at[j, rows], back, lambda slot, rows: gw1_ref.at[rows, half(slot)]
    )

    class Gather:
        def __init__(self, relay, region, place, here, sends, recvs):
            self.relay, self.region, self.place, self.here = relay, region, place, here
            self.sends, self.recvs = sends, recvs

        def move(self, p, step, to):
            j = step % 4
            return copy(
                self.region(p), self.region(p), self.sends.at[j - 1], self.recvs.at[j - 1],
                self.place(at(self.here, to)),
            )

        def start(self):
            if not self.relay:
                self.move(self.here, 2, 2).start()
            self.move(self.here, 1, 1).start()
            self.move(self.here, 3, -1).start()

        def forward(self):
            if self.relay:
                behind = at(self.here, -1)
                self.move(behind, 1, 1).wait_recv()
                self.move(behind, 2, 1).start()

        def wait_recv(self):
            if not self.relay:
                self.move(at(self.here, -1), 1, 1).wait_recv()
            self.move(at(self.here, 1), 3, 1).wait_recv()
            self.move(at(self.here, 2), 2, 1).wait_recv()

        def wait_send(self):
            for j in (1, 2, 3):
                self.move(self.here, j, 1).wait_send()

    class Scatter:
        def __init__(self, relay, source, held, got, place, here, sends, recvs):
            self.relay, self.source, self.held, self.got = relay, source, held, got
            self.place, self.here, self.sends, self.recvs = place, here, sends, recvs

        def move(self, src, step, to):
            j = step % 4
            return copy(
                src, self.got.at[j - 1], self.sends.at[j - 1], self.recvs.at[j - 1],
                self.place(at(self.here, to)),
            )

        def start(self):
            self.move(self.source(at(self.here, 2)), 2, 1 if self.relay else 2).start()
            self.move(self.source(at(self.here, -1)), 3, -1).start()
            if not self.relay:
                self.move(self.source(at(self.here, 1)), 1, 1).start()

        def wait(self, j):
            self.move(self.source(self.here), j, 1).wait_recv()
            return self.got[j - 1].astype(F32)

        def forward(self):
            if self.relay:
                value = self.source(at(self.here, 1))[...].astype(F32) + self.wait(2)
                self.held[...] = value.astype(BF16)
                self.move(self.held, 1, 1).start()

        def total(self, own):
            for j in (3, 1) if self.relay else (1, 3, 2):
                own = own + self.wait(j)
            return own

        def wait_send(self):
            for j in (1, 2, 3):
                self.move(self.source(self.here), j, 1).wait_send()

    def gather_x(i, phase):
        region = (lambda p: ax.at[i, p, y]) if phase == 0 else (lambda p: ax.at[i, :, p])
        place, here = ((on_x, x), (on_y, y))[phase]
        relay = (relay_gather_1, relay_gather_2)[phase]
        return Gather(relay, region, place, here, s_g.at[i, phase, 0], r_g.at[i, phase, 0])

    def gather_c(i, phase):
        region = (lambda p: ac.at[i, x, p]) if phase == 0 else (lambda p: ac.at[i, p])
        place, here = ((on_y, y), (on_x, x))[phase]
        relay = (relay_gather_1, relay_gather_2)[phase]
        return Gather(relay, region, place, here, s_g.at[i, phase, 1], r_g.at[i, phase, 1])

    def gather_h(i):
        return Gather(
            relay_gather_z, lambda p: hg.at[i, :, k, p], on_z, z, s_h.at[i], r_h.at[i]
        )

    def exchange(i, w):
        return copy(ks.at[i, w], kr.at[i, w], s_k.at[i, w], r_k.at[i, w], partner)

    def scatter_z(i, w):
        return Scatter(
            relay_sum_z, lambda p: zs.at[i, w, p], zt.at[i, w], zr.at[i, w], on_z, z,
            s_z.at[i, w], r_z.at[i, w],
        )

    def pair(i, j, p, core):
        return copy(
            hg.at[i, :, core, p], hg.at[i, :, core, p], s_p.at[i, j], r_p.at[i, j], partner
        )

    def scatter_1(i, a):
        source = (lambda p: os.at[i, :, p]) if a == 0 else (lambda p: gs.at[i, p])
        place, here = ((on_y, y), (on_x, x))[a]
        return Scatter(
            relay_sum_1, source, t1.at[i, a], r1.at[i, a], place, here,
            s_o.at[i, 0, a], r_o.at[i, 0, a],
        )

    def scatter_2(i, a):
        place, here = ((on_x, x), (on_y, y))[a]
        return Scatter(
            relay_sum_2, lambda p: u.at[i, a, p], t2.at[i, a], r2.at[i, a], place, here,
            s_o.at[i, 1, a], r_o.at[i, 1, a],
        )

    def gather_1(i):
        gather_x(i, 0).start()
        gather_c(i, 0).start()

    def gather_1_relay(i):
        gather_x(i, 0).forward()
        gather_c(i, 0).forward()

    def gather_2(i):
        gather_x(i, 0).wait_recv()
        gather_x(i, 1).start()
        gather_c(i, 0).wait_recv()
        gather_c(i, 1).start()

    def gather_2_relay(i):
        gather_x(i, 1).forward()
        gather_c(i, 1).forward()

    def give(i, w, product):
        part[i, w] = product.reshape(2, 4, tz, W)
        ks[i, w] = part[i, w, 1 - k]
        exchange(i, w).start()

    def multiply_g(i):
        gather_c(i, 1).wait_recv()
        give(i, 1, dot_nt(ac[i].reshape(n, W), w2_ref[...]))

    def multiply_p(i):
        @pl.when(i == 0)
        def _():
            turn_in.wait_recv()

        gather_x(i, 1).wait_recv()
        give(i, 0, dot_nn(ax[i].reshape(n, W), w1[...].reshape(W, W)))

    def sum_z(i, w):
        exchange(i, w).wait_recv()
        part[i, w, k] += kr[i, w]
        for p in range(4):
            zs[i, w, p] = part[i, w, k, p].astype(BF16)
        scatter_z(i, w).start()

    def sum_z_p(i):
        sum_z(i, 0)

    def sum_z_g(i):
        sum_z(i, 1)

    def sum_z_p_relay(i):
        scatter_z(i, 0).forward()

    def sum_z_g_relay(i):
        scatter_z(i, 1).forward()

    def activate(i):
        grad = scatter_z(i, 1).total(part[i, 1, k, z])
        hidden, slope = activate_both(scatter_z(i, 0).total(part[i, 0, k, z]))
        hg[i, 0, k, z] = hidden.astype(BF16)
        hg[i, 1, k, z] = (grad * slope).astype(BF16)
        gather_h(i).start()
        pair(i, 0, z, k).start()

    def gather_z_relay(i):
        gather_h(i).forward()
        if relay_gather_z:
            pair(i, 1, at(z, -1), k).start()

    def gather_z(i):
        gather_h(i).wait_recv()
        if not relay_gather_z:
            pair(i, 1, at(z, -1), k).start()
        pair(i, 2, at(z, 1), k).start()
        pair(i, 3, at(z, 2), k).start()

    def multiply_2(i):
        pair(i, 0, z, 1 - k).wait_recv()
        pair(i, 1, at(z, 1), 1 - k).wait_recv()
        pair(i, 2, at(z, -1), 1 - k).wait_recv()
        pair(i, 3, at(z, 2), 1 - k).wait_recv()
        product = dot_nn(hg[i, 0].reshape(n, W), w2_ref[...])
        os[i] = product.astype(BF16).reshape(4, 4, m, W)
        scatter_1(i, 0).start()
        product = dot_nt(hg[i, 1].reshape(n, W), w1[...].reshape(W, W))
        gs[i] = product.astype(BF16).reshape(4, 4, m, W)
        scatter_1(i, 1).start()

    def multiply_3(i):
        acc[0] += dot_tn(ax[i].reshape(n, W), hg[i, 1].reshape(n, W))

        @pl.when(i == chunks - 1)
        def _():
            gw1[...] = acc[0].astype(BF16).reshape(2, 256, W)
            turn_out.start()

        acc[1] += dot_tn(hg[i, 0].reshape(n, W), ac[i].reshape(n, W))

    def sum_1_relay(i):
        scatter_1(i, 0).forward()
        scatter_1(i, 1).forward()

    def sum_2(i):
        u[i, 0] = scatter_1(i, 0).total(os[i, :, y].astype(F32)).astype(BF16)
        scatter_2(i, 0).start()
        u[i, 1] = scatter_1(i, 1).total(gs[i, x].astype(F32)).astype(BF16)
        scatter_2(i, 1).start()

    def sum_2_relay(i):
        scatter_2(i, 0).forward()
        scatter_2(i, 1).forward()

    def store(i):
        rows = pl.ds(pl.multiple_of(i * m, m), m)
        out_ref[rows, :] = scatter_2(i, 0).total(u[i, 0, x].astype(F32)).astype(BF16)
        gx_ref[rows, :] = scatter_2(i, 1).total(u[i, 1, y].astype(F32)).astype(BF16)

    def turn_in_relay(i):
        @pl.when(i == 0)
        def _():
            turn_in.forward()

    def turn_out_relay(i):
        @pl.when(i == chunks - 1)
        def _():
            turn_out.forward()

    plan = [
        (14, store),
        (12, sum_2),
        (12, turn_out_relay),
        (10, multiply_2),
        (10, multiply_3),
        (9, gather_z),
        (7, activate),
        (5, sum_z_p),
        (5, sum_z_g),
        (4, multiply_p),
        (4, multiply_g),
        (2, turn_in_relay),
        (2, gather_2),
        (0, gather_1),
    ]

    turn_in.start()

    def tick(now, _):
        for offset, stage in plan:
            i = now - offset

            @pl.when((i >= 0) & (i < chunks))
            def _():
                stage(i)

        return 0

    lax.fori_loop(0, chunks + max(offset for offset, _ in plan), tick, 0)

    gw2_ref[...] = acc[1].astype(BF16)

    def drain(i, _):
        for phase in (0, 1):
            gather_x(i, phase).wait_send()
            gather_c(i, phase).wait_send()
        gather_h(i).wait_send()
        for a in (0, 1):
            exchange(i, a).wait_send()
            scatter_z(i, a).wait_send()
            scatter_1(i, a).wait_send()
            scatter_2(i, a).wait_send()
        for j in range(4):
            pair(i, j, z, k).wait_send()
        return 0

    lax.fori_loop(0, chunks, drain, 0)
    turn_in.wait_send()
    turn_out.wait_recv()
    turn_out.wait_send()


def fused(tokens, cotangent, weight_in, weight_out):
    dma = pltpu.SemaphoreType.DMA
    vmem = pl.BlockSpec(memory_space=pltpu.VMEM)
    anywhere = pl.BlockSpec(memory_space=pl.ANY)
    return pl.pallas_call(
        kernel,
        out_shape=(
            jax.ShapeDtypeStruct((128, W), BF16),
            jax.ShapeDtypeStruct((128, W), BF16),
            jax.ShapeDtypeStruct((256, 2 * W), BF16),
            jax.ShapeDtypeStruct((W, W), BF16),
        ),
        in_specs=[vmem, vmem, anywhere, vmem],
        out_specs=(vmem,) * 4,
        scratch_shapes=[
            pltpu.VMEM((chunks, 4, 4, m, W), BF16),
            pltpu.VMEM((chunks, 4, 4, m, W), BF16),
            pltpu.VMEM((chunks, 2, 2, 4, tz, W), F32),
            pltpu.VMEM((chunks, 2, 4, tz, W), F32),
            pltpu.VMEM((chunks, 2, 4, tz, W), F32),
            pltpu.VMEM((chunks, 2, 4, tz, W), BF16),
            pltpu.VMEM((chunks, 2, tz, W), BF16),
            pltpu.VMEM((chunks, 2, 3, tz, W), BF16),
            pltpu.VMEM((chunks, 2, 2, 4, tz, W), BF16),
            pltpu.VMEM((chunks, 4, 4, m, W), BF16),
            pltpu.VMEM((chunks, 4, 4, m, W), BF16),
            pltpu.VMEM((chunks, 2, 4, m, W), BF16),
            pltpu.VMEM((chunks, 2, 3, 4, m, W), BF16),
            pltpu.VMEM((chunks, 2, 4, m, W), BF16),
            pltpu.VMEM((chunks, 2, m, W), BF16),
            pltpu.VMEM((chunks, 2, 3, m, W), BF16),
            pltpu.VMEM((2, W, W), F32),
            pltpu.VMEM((2, 256, W), BF16),
            pltpu.VMEM((2, 256, W), BF16),
            pltpu.VMEM((2, 256, W), BF16),
            pltpu.VMEM((2, 256, W), BF16),
            dma((chunks, 2, 2, 3)), dma((chunks, 2, 2, 3)),
            dma((chunks, 2)), dma((chunks, 2)),
            dma((chunks, 2, 3)), dma((chunks, 2, 3)),
            dma((chunks, 3)), dma((chunks, 3)),
            dma((chunks, 4)), dma((chunks, 4)),
            dma((chunks, 2, 2, 3)), dma((chunks, 2, 2, 3)),
            dma((2, 2, 2, pieces)), dma((2, 2, 2, pieces)),
        ],
        compiler_params=pltpu.CompilerParams(
            collective_id=0, has_side_effects=True, vmem_limit_bytes=56 << 20
        ),
        cost_estimate=pl.CostEstimate(
            flops=6 * 2 * 2048 * W * W, bytes_accessed=3 << 20, transcendentals=2048 * W
        ),
    )(tokens, cotangent, weight_in, weight_out)


def on_device(tokens, weight_in, weight_out, cotangent):
    return fused(tokens, cotangent, weight_in, weight_out)


def solution(mesh):
    placed = (P("row", "col"),) * 4
    return jax.shard_map(
        on_device, mesh=mesh, in_specs=placed, out_specs=placed, check_vma=False
    )
```

```python
import functools
import math

import jax
import jax.numpy as jnp
from jax import lax
from jax.experimental import pallas as pl
from jax.experimental.pallas import tpu as pltpu
from jax.sharding import PartitionSpec as P

MESH = pl.DeviceIdType.MESH
BF16 = jnp.bfloat16
F32 = jnp.float32

gelu_scale = math.sqrt(2.0 / math.pi)
cubic_term = 0.044715

chunks = 8
m = 128 // chunks
n = 16 * m
tz = n // 8
W = 512
parts_of_result = 2
pieces = 4

relay_gather_1, relay_gather_2 = False, False
relay_sum_z, relay_gather_z = True, True
relay_sum_1, relay_sum_2 = True, False


def activate_both(preact):
    square = preact * preact
    tanh_value = jnp.tanh(gelu_scale * (preact + cubic_term * square * preact))
    half = 0.5 * (1.0 + tanh_value)
    slope = half + 0.5 * preact * (1.0 - tanh_value * tanh_value) * gelu_scale * (
        1.0 + 3.0 * cubic_term * square
    )
    return preact * half, slope


def dot_nn(left, right):
    return jnp.dot(left, right, preferred_element_type=F32)


def dot_nt(left, right):
    return lax.dot_general(
        left, right, (((1,), (1,)), ((), ())), preferred_element_type=F32
    )


def dot_tn(left, right):
    return lax.dot_general(
        left, right, (((0,), (0,)), ((), ())), preferred_element_type=F32
    )


def kernel(
    x_ref, c_ref, win_ref, wout_ref,
    out_ref, gx_ref, gw1_ref, gw2_ref,
    ax, ac, part, ks, kr, zs, zt, zr, hg, os, gs, t1, r1, u, t2, r2, acc,
    w1, w2, gw1, gw2, stay, back, ready,
    s_g, r_g, s_k, r_k, s_z, r_z, s_h, r_h, s_p, r_p, s_o, r_o, s_w, r_w, s_l, r_l,
):
    row, col = lax.axis_index("row"), lax.axis_index("col")
    x, y, z, k = row // 4, lax.rem(row, 4), col // 2, lax.rem(col, 2)
    sign = 1 - 2 * k

    def at(base, step):
        return lax.rem(base + step * sign + 4, 4)

    def on_x(p):
        return (p * 4 + y, col)

    def on_y(p):
        return (x * 4 + p, col)

    def on_z(p):
        return (row, p * 2 + k)

    partner = (row, z * 2 + 1 - k)

    def copy(src, dst, send, recv, device):
        return pltpu.make_async_remote_copy(
            src_ref=src, dst_ref=dst, send_sem=send, recv_sem=recv,
            device_id=device, device_id_type=MESH,
        )

    def shift(b):
        return lax.rem(b + x + y, 4)

    def turn_target(b):
        return (lax.rem(z - shift(b) + 4, 4) * 4 + b, x * 2 + y // 2)

    def turn_source(slot):
        return (z * 4 + 2 * k + slot, lax.rem(x + y + z + 2 * k + slot, 4) * 2 + y // 2)

    home = (x == z) & (lax.rem(x + 2 * y, 4) == 0) & (k == y // 2)

    def is_home(j):
        return home & (lax.rem(y, 2) == j)

    barrier = pltpu.get_barrier_semaphore()

    def greet(device):
        pl.semaphore_signal(barrier, inc=1, device_id=device, device_id_type=MESH)

    for j in (1, 2, 3):
        greet(on_x(lax.rem(x + j, 4)))
        greet(on_y(lax.rem(y + j, 4)))
        greet(on_z(lax.rem(z + j, 4)))
    greet(partner)
    for j in (0, 1):

        @pl.when(jnp.logical_not(is_home(j)))
        def _():
            greet(turn_target(2 * k + j))
            greet(turn_source(j))

    loads = [
        pltpu.make_async_copy(x_ref, ax.at[:, x, y], s_l.at[0]),
        pltpu.make_async_copy(c_ref, ac.at[:, x, y], s_l.at[1]),
        pltpu.make_async_copy(wout_ref, w2, s_l.at[2]),
    ]
    for one in loads:
        one.start()
    acc[...] = jnp.zeros_like(acc)
    loads[0].wait()
    loads[1].wait()
    pl.semaphore_wait(barrier, 14 - 2 * home.astype(jnp.int32))

    size = 256 // pieces

    class Turn:
        def __init__(self, way, source, middle, target):
            self.way, self.source, self.middle, self.target = way, source, middle, target

        def move_1(self, j, q):
            where = (self.way, 0, j, q)
            rows = pl.ds(q * size, size)
            return copy(
                self.source(j, rows), self.middle.at[j, rows], s_w.at[where], r_w.at[where],
                on_z(lax.rem(z + shift(2 * k + j), 4)),
            )

        def move_2(self, j, q, slot):
            send, recv = (self.way, 1, j, q), (self.way, 1, slot, q)
            rows = pl.ds(q * size, size)
            return copy(
                self.middle.at[j, rows], self.target(slot, rows),
                s_w.at[send], r_w.at[recv], turn_target(2 * k + j),
            )

        def stay_1(self, j, q):
            rows = pl.ds(q * size, size)
            return pltpu.make_async_copy(
                self.source(j, rows), self.middle.at[j, rows], r_w.at[self.way, 0, j, q]
            )

        def stay_2(self, j, q):
            rows = pl.ds(q * size, size)
            return pltpu.make_async_copy(
                self.middle.at[j, rows], self.target(j, rows), r_w.at[self.way, 1, j, q]
            )

        def either(self, condition, yes, no):
            pl.when(condition)(yes)
            pl.when(jnp.logical_not(condition))(no)

        def start(self):
            for q in range(pieces):
                for j in (0, 1):
                    self.either(
                        shift(2 * k + j) == 0,
                        lambda: self.stay_1(j, q).start(),
                        lambda: self.move_1(j, q).start(),
                    )

        def forward(self):
            slot = lax.rem(y, 2)
            for q in range(pieces):
                for j in (0, 1):
                    self.move_1(j, q).wait_recv()
                    self.either(
                        is_home(j),
                        lambda: self.stay_2(j, q).start(),
                        lambda: self.move_2(j, q, slot).start(),
                    )

        def wait_recv(self):
            for q in range(pieces):
                for slot in (0, 1):
                    self.move_2(0, q, slot).wait_recv()

        def wait_send(self):
            for q in range(pieces):
                for j in (0, 1):
                    pl.when(shift(2 * k + j) != 0)(lambda: self.move_1(j, q).wait_send())
                    pl.when(jnp.logical_not(is_home(j)))(
                        lambda: self.move_2(j, q, 0).wait_send()
                    )

    def half(slot):
        return pl.ds(pl.multiple_of(slot * W, W), W)

    turn_in = Turn(
        0, lambda j, rows: win_ref.at[rows, half(j)], stay, lambda slot, rows: w1.at[slot, rows]
    )
    turn_out = Turn(
        1, lambda j, rows: gw1.at[j, rows], back, lambda slot, rows: gw1_ref.at[rows, half(slot)]
    )

    class Gather:
        def __init__(self, relay, region, place, here, sends, recvs):
            self.relay, self.region, self.place, self.here = relay, region, place, here
            self.sends, self.recvs = sends, recvs

        def move(self, p, step, to):
            j = step % 4
            return copy(
                self.region(p), self.region(p), self.sends.at[j - 1], self.recvs.at[j - 1],
                self.place(at(self.here, to)),
            )

        def start(self):
            if not self.relay:
                self.move(self.here, 2, 2).start()
            self.move(self.here, 1, 1).start()
            self.move(self.here, 3, -1).start()

        def forward(self):
            if self.relay:
                behind = at(self.here, -1)
                self.move(behind, 1, 1).wait_recv()
                self.move(behind, 2, 1).start()

        def wait_recv(self):
            if not self.relay:
                self.move(at(self.here, -1), 1, 1).wait_recv()
            self.move(at(self.here, 1), 3, 1).wait_recv()
            self.move(at(self.here, 2), 2, 1).wait_recv()

        def wait_send(self):
            for j in (1, 2, 3):
                self.move(self.here, j, 1).wait_send()

    class Scatter:
        def __init__(self, relay, source, held, got, place, here, sends, recvs):
            self.relay, self.source, self.held, self.got = relay, source, held, got
            self.place, self.here, self.sends, self.recvs = place, here, sends, recvs

        def move(self, src, step, to):
            j = step % 4
            return copy(
                src, self.got.at[j - 1], self.sends.at[j - 1], self.recvs.at[j - 1],
                self.place(at(self.here, to)),
            )

        def start(self):
            self.move(self.source(at(self.here, 2)), 2, 1 if self.relay else 2).start()
            self.move(self.source(at(self.here, -1)), 3, -1).start()
            if not self.relay:
                self.move(self.source(at(self.here, 1)), 1, 1).start()

        def wait(self, j):
            self.move(self.source(self.here), j, 1).wait_recv()
            return self.got[j - 1].astype(F32)

        def forward(self):
            if self.relay:
                value = self.source(at(self.here, 1))[...].astype(F32) + self.wait(2)
                self.held[...] = value.astype(BF16)
                self.move(self.held, 1, 1).start()

        def total(self, own):
            for j in (3, 1) if self.relay else (1, 3, 2):
                own = own + self.wait(j)
            return own

        def wait_send(self):
            for j in (1, 2, 3):
                self.move(self.source(self.here), j, 1).wait_send()

    def gather_x(i, phase):
        region = (lambda p: ax.at[i, p, y]) if phase == 0 else (lambda p: ax.at[i, :, p])
        place, here = ((on_x, x), (on_y, y))[phase]
        relay = (relay_gather_1, relay_gather_2)[phase]
        return Gather(relay, region, place, here, s_g.at[i, phase, 0], r_g.at[i, phase, 0])

    def gather_c(i, phase):
        region = (lambda p: ac.at[i, x, p]) if phase == 0 else (lambda p: ac.at[i, p])
        place, here = ((on_y, y), (on_x, x))[phase]
        relay = (relay_gather_1, relay_gather_2)[phase]
        return Gather(relay, region, place, here, s_g.at[i, phase, 1], r_g.at[i, phase, 1])

    def gather_h(i):
        return Gather(
            relay_gather_z, lambda p: hg.at[i, :, k, p], on_z, z, s_h.at[i], r_h.at[i]
        )

    def exchange(i, w):
        return copy(ks.at[i, w], kr.at[i, w], s_k.at[i, w], r_k.at[i, w], partner)

    def scatter_z(i, w):
        return Scatter(
            relay_sum_z, lambda p: zs.at[i, w, p], zt.at[i, w], zr.at[i, w], on_z, z,
            s_z.at[i, w], r_z.at[i, w],
        )

    def pair(i, j, p, core):
        return copy(
            hg.at[i, :, core, p], hg.at[i, :, core, p], s_p.at[i, j], r_p.at[i, j], partner
        )

    def scatter_1(i, a):
        source = (lambda p: os.at[i, :, p]) if a == 0 else (lambda p: gs.at[i, p])
        place, here = ((on_y, y), (on_x, x))[a]
        return Scatter(
            relay_sum_1, source, t1.at[i, a], r1.at[i, a], place, here,
            s_o.at[i, 0, a], r_o.at[i, 0, a],
        )

    def scatter_2(i, a):
        place, here = ((on_x, x), (on_y, y))[a]
        return Scatter(
            relay_sum_2, lambda p: u.at[i, a, p], t2.at[i, a], r2.at[i, a], place, here,
            s_o.at[i, 1, a], r_o.at[i, 1, a],
        )

    def gather_1x(i):
        gather_x(i, 0).start()

    def gather_1c(i):
        gather_c(i, 0).start()

    def gather_2x(i):
        gather_x(i, 0).wait_recv()
        gather_x(i, 1).start()

    def gather_2c(i):
        gather_c(i, 0).wait_recv()
        gather_c(i, 1).start()

    def gather_2x_relay(i):
        gather_x(i, 1).forward()

    def gather_2c_relay(i):
        gather_c(i, 1).forward()

    def give(i, w, product):
        part[i, w] = product.reshape(2, 4, tz, W)
        ks[i, w] = part[i, w, 1 - k]
        exchange(i, w).start()

    def multiply_g(i):
        @pl.when(i == 0)
        def _():
            loads[2].wait()

        gather_c(i, 1).wait_recv()
        give(i, 1, dot_nt(ac[i].reshape(n, W), w2[...]))

    def multiply_p(i):
        @pl.when(i == 0)
        def _():
            turn_in.wait_recv()

        gather_x(i, 1).wait_recv()
        give(i, 0, dot_nn(ax[i].reshape(n, W), w1[...].reshape(W, W)))

    def sum_z(i, w):
        exchange(i, w).wait_recv()
        part[i, w, k] += kr[i, w]
        for p in range(4):
            zs[i, w, p] = part[i, w, k, p].astype(BF16)
        scatter_z(i, w).start()

    def sum_z_p(i):
        sum_z(i, 0)

    def sum_z_g(i):
        sum_z(i, 1)

    def sum_z_p_relay(i):
        scatter_z(i, 0).forward()

    def sum_z_g_relay(i):
        scatter_z(i, 1).forward()

    def activate(i):
        grad = scatter_z(i, 1).total(part[i, 1, k, z])
        hidden, slope = activate_both(scatter_z(i, 0).total(part[i, 0, k, z]))
        hg[i, 0, k, z] = hidden.astype(BF16)
        hg[i, 1, k, z] = (grad * slope).astype(BF16)
        gather_h(i).start()
        pair(i, 0, z, k).start()

    def gather_z_relay(i):
        gather_h(i).forward()
        if relay_gather_z:
            pair(i, 1, at(z, -1), k).start()

    def gather_z(i):
        gather_h(i).wait_recv()
        if not relay_gather_z:
            pair(i, 1, at(z, -1), k).start()
        pair(i, 2, at(z, 1), k).start()
        pair(i, 3, at(z, 2), k).start()

    def multiply_w(i):
        pair(i, 0, z, 1 - k).wait_recv()
        pair(i, 1, at(z, 1), 1 - k).wait_recv()
        pair(i, 2, at(z, -1), 1 - k).wait_recv()
        pair(i, 3, at(z, 2), 1 - k).wait_recv()
        acc[0] += dot_tn(ax[i].reshape(n, W), hg[i, 1].reshape(n, W))

        @pl.when(i == chunks - 1)
        def _():
            gw1[...] = acc[0].astype(BF16).reshape(2, 256, W)
            turn_out.start()

    def multiply_o(i):
        product = dot_nn(hg[i, 0].reshape(n, W), w2[...])
        os[i] = product.astype(BF16).reshape(4, 4, m, W)
        scatter_1(i, 0).start()

    def multiply_x(i):
        product = dot_nt(hg[i, 1].reshape(n, W), w1[...].reshape(W, W))
        gs[i] = product.astype(BF16).reshape(4, 4, m, W)
        scatter_1(i, 1).start()

    def multiply_v(i):
        acc[1] += dot_tn(hg[i, 0].reshape(n, W), ac[i].reshape(n, W))

    def sum_1o_relay(i):
        scatter_1(i, 0).forward()

    def sum_1x_relay(i):
        scatter_1(i, 1).forward()

    def sum_2o(i):
        u[i, 0] = scatter_1(i, 0).total(os[i, :, y].astype(F32)).astype(BF16)
        scatter_2(i, 0).start()

    def sum_2x(i):
        u[i, 1] = scatter_1(i, 1).total(gs[i, x].astype(F32)).astype(BF16)
        scatter_2(i, 1).start()

    def keep(i, a):
        return pltpu.make_async_copy(ready.at[a, i], (out_ref, gx_ref)[a].at[i], r_l.at[a, i])

    def store_o(i):
        ready[0, i] = scatter_2(i, 0).total(u[i, 0, x].astype(F32)).astype(BF16)
        keep(i, 0).start()

    def store_x(i):
        ready[1, i] = scatter_2(i, 1).total(u[i, 1, y].astype(F32)).astype(BF16)
        keep(i, 1).start()

    def turn_in_relay(i):
        @pl.when(i == 0)
        def _():
            turn_in.forward()

    def turn_out_relay(i):
        @pl.when(i == chunks - 1)
        def _():
            turn_out.forward()

    plan = [
        (17, multiply_o),
        (17, multiply_x),
        (11, sum_z_g_relay),
        (14, gather_z_relay),
        (24, multiply_v),
        (1, gather_1x),
        (25, sum_2o),
        (16, multiply_w),
        (19, sum_1o_relay),
        (12, activate),
        (9, multiply_p),
        (24, sum_2x),
        (9, multiply_g),
        (41, store_o),
        (19, sum_1x_relay),
        (20, turn_out_relay),
        (6, gather_2x),
        (9, sum_z_p),
        (9, sum_z_g),
        (37, store_x),
        (15, gather_z),
        (1, gather_1c),
        (10, sum_z_p_relay),
        (6, gather_2c),
        (6, turn_in_relay),
    ]

    turn_in.start()

    def tick(now, _):
        for offset, stage in plan:
            i = now - offset

            @pl.when((i >= 0) & (i < chunks))
            def _():
                stage(i)

        return 0

    lax.fori_loop(0, chunks + max(offset for offset, _ in plan), tick, 0)

    keep_w = pltpu.make_async_copy(gw2, gw2_ref, s_l.at[3])
    gw2[...] = acc[1].astype(BF16)
    keep_w.start()

    def drain(i, _):
        for phase in (0, 1):
            gather_x(i, phase).wait_send()
            gather_c(i, phase).wait_send()
        gather_h(i).wait_send()
        for a in (0, 1):
            keep(i, a).wait()
            exchange(i, a).wait_send()
            scatter_z(i, a).wait_send()
            scatter_1(i, a).wait_send()
            scatter_2(i, a).wait_send()
        for j in range(4):
            pair(i, j, z, k).wait_send()
        return 0

    lax.fori_loop(0, chunks, drain, 0)
    turn_in.wait_send()
    turn_out.wait_recv()
    turn_out.wait_send()
    keep_w.wait()


def fused(tokens, cotangent, weight_in, weight_out):
    dma = pltpu.SemaphoreType.DMA
    anywhere = pl.BlockSpec(memory_space=pl.ANY)
    return pl.pallas_call(
        kernel,
        out_shape=(
            jax.ShapeDtypeStruct((chunks, m, W), BF16),
            jax.ShapeDtypeStruct((chunks, m, W), BF16),
            jax.ShapeDtypeStruct((256, 2 * W), BF16),
            jax.ShapeDtypeStruct((W, W), BF16),
        ),
        in_specs=[anywhere] * 4,
        out_specs=(anywhere,) * 4,
        scratch_shapes=[
            pltpu.VMEM((chunks, 4, 4, m, W), BF16),
            pltpu.VMEM((chunks, 4, 4, m, W), BF16),
            pltpu.VMEM((chunks, 2, 2, 4, tz, W), F32),
            pltpu.VMEM((chunks, 2, 4, tz, W), F32),
            pltpu.VMEM((chunks, 2, 4, tz, W), F32),
            pltpu.VMEM((chunks, 2, 4, tz, W), BF16),
            pltpu.VMEM((chunks, 2, tz, W), BF16),
            pltpu.VMEM((chunks, 2, 3, tz, W), BF16),
            pltpu.VMEM((chunks, 2, 2, 4, tz, W), BF16),
            pltpu.VMEM((chunks, 4, 4, m, W), BF16),
            pltpu.VMEM((chunks, 4, 4, m, W), BF16),
            pltpu.VMEM((chunks, 2, 4, m, W), BF16),
            pltpu.VMEM((chunks, 2, 3, 4, m, W), BF16),
            pltpu.VMEM((chunks, 2, 4, m, W), BF16),
            pltpu.VMEM((chunks, 2, m, W), BF16),
            pltpu.VMEM((chunks, 2, 3, m, W), BF16),
            pltpu.VMEM((2, W, W), F32),
            pltpu.VMEM((2, 256, W), BF16),
            pltpu.VMEM((W, W), BF16),
            pltpu.VMEM((2, 256, W), BF16),
            pltpu.VMEM((W, W), BF16),
            pltpu.VMEM((2, 256, W), BF16),
            pltpu.VMEM((2, 256, W), BF16),
            pltpu.VMEM((2, chunks, m, W), BF16),
            dma((chunks, 2, 2, 3)), dma((chunks, 2, 2, 3)),
            dma((chunks, 2)), dma((chunks, 2)),
            dma((chunks, 2, 3)), dma((chunks, 2, 3)),
            dma((chunks, 3)), dma((chunks, 3)),
            dma((chunks, 4)), dma((chunks, 4)),
            dma((chunks, 2, 2, 3)), dma((chunks, 2, 2, 3)),
            dma((2, 2, 2, pieces)), dma((2, 2, 2, pieces)),
            dma((4,)), dma((2, chunks)),
        ],
        compiler_params=pltpu.CompilerParams(
            collective_id=0, has_side_effects=True, vmem_limit_bytes=56 << 20
        ),
        cost_estimate=pl.CostEstimate(
            flops=6 * 2 * 2048 * W * W, bytes_accessed=3 << 20, transcendentals=2048 * W
        ),
    )(tokens.reshape(chunks, m, W), cotangent.reshape(chunks, m, W), weight_in, weight_out)


def hand_over(*refs):
    held, given, rooms, arrived, done = refs[:4], refs[4:8], refs[8:12], refs[12], refs[13]
    ways = []
    for i in range(4):
        rows = held[i].shape[0] // parts_of_result
        for j in range(parts_of_result):
            part = pl.ds(j * rows, rows)
            room = rooms[i].at[part]
            ways.append((
                pltpu.make_async_copy(held[i].at[part], room, arrived.at[i, j]),
                pltpu.make_async_copy(room, given[i].at[part], done.at[i, j]),
            ))
    for come, _ in ways:
        come.start()
    for come, go in ways:
        come.wait()
        go.start()
    for _, go in ways:
        go.wait()


def on_device(tokens, weight_in, weight_out, cotangent):
    output, grad_tokens, grad_in, grad_out = fused(tokens, cotangent, weight_in, weight_out)
    results = (output.reshape(128, W), grad_tokens.reshape(128, W), grad_in, grad_out)
    anywhere = pl.BlockSpec(memory_space=pl.ANY)
    return pl.pallas_call(
        hand_over,
        out_shape=[jax.ShapeDtypeStruct(r.shape, r.dtype) for r in results],
        in_specs=[anywhere] * 4,
        out_specs=[anywhere] * 4,
        scratch_shapes=[pltpu.VMEM(r.shape, r.dtype) for r in results]
        + [pltpu.SemaphoreType.DMA((4, parts_of_result))] * 2,
    )(*results)


def solution(mesh):
    placed = (P("row", "col"),) * 4
    return jax.shard_map(
        on_device, mesh=mesh, in_specs=placed, out_specs=placed, check_vma=False
    )
```

```python
import functools
import math

import jax
import jax.numpy as jnp
from jax import lax
from jax.experimental import pallas as pl
from jax.experimental.pallas import tpu as pltpu
from jax.sharding import PartitionSpec as P

MESH = pl.DeviceIdType.MESH
BF16 = jnp.bfloat16
F32 = jnp.float32

gelu_scale = math.sqrt(2.0 / math.pi)
cubic_term = 0.044715

chunks = 8
m = 128 // chunks
n = 16 * m
tz = n // 8
W = 512
parts_of_result = 2
pieces = 4

relay_gather_1, relay_gather_2 = False, False
relay_sum_z, relay_gather_z = True, True
relay_sum_1, relay_sum_2 = True, False


def activate_both(preact):
    square = preact * preact
    tanh_value = jnp.tanh(gelu_scale * (preact + cubic_term * square * preact))
    half = 0.5 * (1.0 + tanh_value)
    slope = half + 0.5 * preact * (1.0 - tanh_value * tanh_value) * gelu_scale * (
        1.0 + 3.0 * cubic_term * square
    )
    return preact * half, slope


def dot_nn(left, right):
    return jnp.dot(left, right, preferred_element_type=F32)


def dot_nt(left, right):
    return lax.dot_general(
        left, right, (((1,), (1,)), ((), ())), preferred_element_type=F32
    )


def dot_tn(left, right):
    return lax.dot_general(
        left, right, (((0,), (0,)), ((), ())), preferred_element_type=F32
    )


def kernel(
    x_ref, c_ref, win_ref, wout_ref,
    out_ref, gx_ref, gw1_ref, gw2_ref,
    ax, ac, part, kr, zs, zt, zr, hg, os, gs, t1, r1, u, t2, r2, acc,
    w1, w2, gw1, gw2, stay, back, ready,
    s_g, r_g, s_k, r_k, s_z, r_z, s_h, r_h, s_p, r_p, s_o, r_o, r_q, s_w, r_w, r_t, s_l, r_l,
):
    row, col = lax.axis_index("row"), lax.axis_index("col")
    x, y, z, k = row // 4, lax.rem(row, 4), col // 2, lax.rem(col, 2)
    sign = 1 - 2 * k

    def at(base, step):
        return lax.rem(base + step * sign + 4, 4)

    def on_x(p):
        return (p * 4 + y, col)

    def on_y(p):
        return (x * 4 + p, col)

    def on_z(p):
        return (row, p * 2 + k)

    partner = (row, z * 2 + 1 - k)

    def copy(src, dst, send, recv, device):
        return pltpu.make_async_remote_copy(
            src_ref=src, dst_ref=dst, send_sem=send, recv_sem=recv,
            device_id=device, device_id_type=MESH,
        )

    def shift(b):
        return lax.rem(b + x + y, 4)

    def turn_target(b):
        return (lax.rem(z - shift(b) + 4, 4) * 4 + b, x * 2 + y // 2)

    def turn_source(slot):
        return (z * 4 + 2 * k + slot, lax.rem(x + y + z + 2 * k + slot, 4) * 2 + y // 2)

    home = (x == z) & (lax.rem(x + 2 * y, 4) == 0) & (k == y // 2)

    def is_home(j):
        return home & (lax.rem(y, 2) == j)

    barrier = pltpu.get_barrier_semaphore()

    def greet(device):
        pl.semaphore_signal(barrier, inc=1, device_id=device, device_id_type=MESH)

    for j in (1, 2, 3):
        greet(on_x(lax.rem(x + j, 4)))
        greet(on_y(lax.rem(y + j, 4)))
        greet(on_z(lax.rem(z + j, 4)))
    greet(partner)
    for j in (0, 1):

        @pl.when(jnp.logical_not(is_home(j)))
        def _():
            greet(turn_target(2 * k + j))
            greet(turn_source(j))

    loads = [
        pltpu.make_async_copy(x_ref, ax.at[:, x, y], s_l.at[0]),
        pltpu.make_async_copy(c_ref, ac.at[:, x, y], s_l.at[1]),
        pltpu.make_async_copy(wout_ref, w2, s_l.at[2]),
    ]
    for one in loads:
        one.start()
    acc[...] = jnp.zeros_like(acc)
    loads[0].wait()
    loads[1].wait()
    pl.semaphore_wait(barrier, 14 - 2 * home.astype(jnp.int32))

    size = 256 // pieces

    class Turn:
        def __init__(self, way, source, middle, target):
            self.way, self.source, self.middle, self.target = way, source, middle, target

        def move_1(self, j, q):
            where = (self.way, j, q)
            rows = pl.ds(q * size, size)
            return copy(
                self.source(j, rows), self.middle.at[j, rows], s_w.at[self.way, 0, j], r_w.at[where],
                on_z(lax.rem(z + shift(2 * k + j), 4)),
            )

        def move_2(self, j, q, slot):
            rows = pl.ds(q * size, size)
            return copy(
                self.middle.at[j, rows], self.target(slot, rows),
                s_w.at[self.way, 1, j], r_t.at[self.way], turn_target(2 * k + j),
            )

        def stay_1(self, j, q):
            rows = pl.ds(q * size, size)
            return pltpu.make_async_copy(
                self.source(j, rows), self.middle.at[j, rows], r_w.at[self.way, j, q]
            )

        def stay_2(self, j, q):
            rows = pl.ds(q * size, size)
            return pltpu.make_async_copy(
                self.middle.at[j, rows], self.target(j, rows), r_t.at[self.way]
            )

        def either(self, condition, yes, no):
            pl.when(condition)(yes)
            pl.when(jnp.logical_not(condition))(no)

        def start(self):
            for q in range(pieces):
                for j in (0, 1):
                    self.either(
                        shift(2 * k + j) == 0,
                        lambda: self.stay_1(j, q).start(),
                        lambda: self.move_1(j, q).start(),
                    )

        def forward(self):
            slot = lax.rem(y, 2)
            for q in range(pieces):
                for j in (0, 1):
                    self.move_1(j, q).wait_recv()
                    self.either(
                        is_home(j),
                        lambda: self.stay_2(j, q).start(),
                        lambda: self.move_2(j, q, slot).start(),
                    )

        def whole(self, j, stage):
            return copy(
                self.middle.at[j], self.middle.at[j], s_w.at[self.way, stage, j],
                r_t.at[self.way], partner,
            )

        def wait_recv(self):
            copy(
                self.middle, self.middle, s_w.at[self.way, 0, 0], r_t.at[self.way], partner
            ).wait_recv()

        def wait_send(self):
            for j in (0, 1):
                pl.when(shift(2 * k + j) != 0)(lambda: self.whole(j, 0).wait_send())
                pl.when(jnp.logical_not(is_home(j)))(lambda: self.whole(j, 1).wait_send())

    def half(slot):
        return pl.ds(pl.multiple_of(slot * W, W), W)

    turn_in = Turn(
        0, lambda j, rows: win_ref.at[rows, half(j)], stay, lambda slot, rows: w1.at[slot, rows]
    )
    turn_out = Turn(
        1, lambda j, rows: gw1.at[j, rows], back, lambda slot, rows: gw1_ref.at[rows, half(slot)]
    )

    class Gather:
        def __init__(self, relay, region, place, here, send, recvs):
            self.relay, self.region, self.place, self.here = relay, region, place, here
            self.send, self.recvs = send, recvs

        def move(self, p, step, to):
            first = self.relay and step == 1
            return copy(
                self.region(p), self.region(p), self.send, self.recvs.at[1 if first else 0],
                self.place(at(self.here, to)),
            )

        def start(self):
            if not self.relay:
                self.move(self.here, 2, 2).start()
            self.move(self.here, 1, 1).start()
            self.move(self.here, 3, -1).start()

        def forward(self):
            if self.relay:
                behind = at(self.here, -1)
                self.move(behind, 1, 1).wait_recv()
                self.move(behind, 2, 1).start()

        def wait_recv(self):
            blocks = self.region(pl.ds(0, 2 if self.relay else 3))
            copy(blocks, blocks, self.send, self.recvs.at[0], partner).wait_recv()

    class Scatter:
        def __init__(self, relay, source, held, got, place, here, send, recvs):
            self.relay, self.source, self.held, self.got = relay, source, held, got
            self.place, self.here, self.send, self.recvs = place, here, send, recvs

        def move(self, src, step, to):
            slot = {2: 0, 3: 1, 1: 2}[step]
            first = self.relay and step == 2
            return copy(
                src, self.got.at[slot], self.send, self.recvs.at[1 if first else 0],
                self.place(at(self.here, to)),
            )

        def start(self):
            self.move(self.source(at(self.here, 2)), 2, 1 if self.relay else 2).start()
            self.move(self.source(at(self.here, -1)), 3, -1).start()
            if not self.relay:
                self.move(self.source(at(self.here, 1)), 1, 1).start()

        def forward(self, own):
            if self.relay:
                self.move(self.source(self.here), 2, 1).wait_recv()
                self.held[...] = (own + self.got[0].astype(F32)).astype(BF16)
                self.move(self.held, 1, 1).start()

        def total(self, own):
            blocks = self.got.at[pl.ds(1, 2)] if self.relay else self.got
            copy(blocks, blocks, self.send, self.recvs.at[0], partner).wait_recv()
            for slot in (1, 2) if self.relay else (0, 1, 2):
                own = own + self.got[slot].astype(F32)
            return own

    def gather_x(i, phase):
        region = (lambda p: ax.at[i, p, y]) if phase == 0 else (lambda p: ax.at[i, :, p])
        place, here = ((on_x, x), (on_y, y))[phase]
        relay = (relay_gather_1, relay_gather_2)[phase]
        return Gather(relay, region, place, here, s_g.at[phase, 0], r_g.at[i, phase, 0])

    def gather_c(i, phase):
        region = (lambda p: ac.at[i, x, p]) if phase == 0 else (lambda p: ac.at[i, p])
        place, here = ((on_y, y), (on_x, x))[phase]
        relay = (relay_gather_1, relay_gather_2)[phase]
        return Gather(relay, region, place, here, s_g.at[phase, 1], r_g.at[i, phase, 1])

    def gather_h(i):
        return Gather(
            relay_gather_z, lambda p: hg.at[i, :, k, p], on_z, z, s_h.at[0], r_h.at[i]
        )

    def exchange(i, w):
        return copy(part.at[i, w, 1 - k], kr.at[i, w], s_k.at[w], r_k.at[i, w], partner)

    def scatter_z(i, w):
        return Scatter(
            relay_sum_z, lambda p: zs.at[i, w, p], zt.at[i, w], zr.at[i, w], on_z, z,
            s_z.at[w], r_z.at[i, w],
        )

    def pair(i, p):
        return copy(
            hg.at[i, :, k, p], hg.at[i, :, k, p], s_p.at[0], r_p.at[i], partner
        )

    def scatter_1(i, a):
        source = (lambda p: os.at[i, :, p]) if a == 0 else (lambda p: gs.at[i, p])
        place, here = ((on_y, y), (on_x, x))[a]
        return Scatter(
            relay_sum_1, source, t1.at[i, a], r1.at[i, a], place, here,
            s_o.at[0, a], r_o.at[i, a],
        )

    def scatter_2(i, a):
        place, here = ((on_x, x), (on_y, y))[a]
        return Scatter(
            relay_sum_2, lambda p: u.at[i, a, p], t2.at[i, a], r2.at[i, a], place, here,
            s_o.at[1, a], r_q.at[i, pl.ds(a, 1)],
        )

    def gather_1x(i):
        gather_x(i, 0).start()

    def gather_1c(i):
        gather_c(i, 0).start()

    def gather_2x(i):
        gather_x(i, 0).wait_recv()
        gather_x(i, 1).start()

    def gather_2c(i):
        gather_c(i, 0).wait_recv()
        gather_c(i, 1).start()

    def gather_2x_relay(i):
        gather_x(i, 1).forward()

    def gather_2c_relay(i):
        gather_c(i, 1).forward()

    def give(i, w, product):
        part[i, w] = product.reshape(2, 4, tz, W)
        exchange(i, w).start()

    def mixed(i, w, p):
        return part[i, w, k, p] + kr[i, w, p]

    def multiply_g(i):
        @pl.when(i == 0)
        def _():
            loads[2].wait()

        gather_c(i, 1).wait_recv()
        give(i, 1, dot_nt(ac[i].reshape(n, W), w2[...]))

    def multiply_p(i):
        @pl.when(i == 0)
        def _():
            turn_in.wait_recv()

        gather_x(i, 1).wait_recv()
        give(i, 0, dot_nn(ax[i].reshape(n, W), w1[...].reshape(W, W)))

    def sum_z(i, w):
        exchange(i, w).wait_recv()
        for p in range(4):
            zs[i, w, p] = mixed(i, w, p).astype(BF16)
        scatter_z(i, w).start()

    def sum_z_p(i):
        sum_z(i, 0)

    def sum_z_g(i):
        sum_z(i, 1)

    def sum_z_p_relay(i):
        scatter_z(i, 0).forward(mixed(i, 0, at(z, 1)))

    def sum_z_g_relay(i):
        scatter_z(i, 1).forward(mixed(i, 1, at(z, 1)))

    def activate(i):
        grad = scatter_z(i, 1).total(mixed(i, 1, z))
        hidden, slope = activate_both(scatter_z(i, 0).total(mixed(i, 0, z)))
        hg[i, 0, k, z] = hidden.astype(BF16)
        hg[i, 1, k, z] = (grad * slope).astype(BF16)
        gather_h(i).start()
        pair(i, z).start()

    def gather_z_relay(i):
        gather_h(i).forward()
        if relay_gather_z:
            pair(i, at(z, -1)).start()

    def gather_z(i):
        gather_h(i).wait_recv()
        if not relay_gather_z:
            pair(i, at(z, -1)).start()
        pair(i, at(z, 1)).start()
        pair(i, at(z, 2)).start()

    def multiply_w(i):
        others = hg.at[i, :, 1 - k]
        copy(others, others, s_p.at[0], r_p.at[i], partner).wait_recv()
        acc[0] += dot_tn(ax[i].reshape(n, W), hg[i, 1].reshape(n, W))

        @pl.when(i == chunks - 1)
        def _():
            gw1[...] = acc[0].astype(BF16).reshape(2, 256, W)
            turn_out.start()

    def multiply_o(i):
        product = dot_nn(hg[i, 0].reshape(n, W), w2[...])
        os[i] = product.astype(BF16).reshape(4, 4, m, W)
        scatter_1(i, 0).start()

    def multiply_x(i):
        product = dot_nt(hg[i, 1].reshape(n, W), w1[...].reshape(W, W))
        gs[i] = product.astype(BF16).reshape(4, 4, m, W)
        scatter_1(i, 1).start()

    def multiply_v(i):
        acc[1] += dot_tn(hg[i, 0].reshape(n, W), ac[i].reshape(n, W))

    def sum_1o_relay(i):
        scatter_1(i, 0).forward(os[i, :, at(y, 1)].astype(F32))

    def sum_1x_relay(i):
        scatter_1(i, 1).forward(gs[i, at(x, 1)].astype(F32))

    def sum_2o(i):
        u[i, 0] = scatter_1(i, 0).total(os[i, :, y].astype(F32)).astype(BF16)
        scatter_2(i, 0).start()

    def sum_2x(i):
        u[i, 1] = scatter_1(i, 1).total(gs[i, x].astype(F32)).astype(BF16)
        scatter_2(i, 1).start()

    def keep(i, a):
        return pltpu.make_async_copy(ready.at[a, i], (out_ref, gx_ref)[a].at[i], r_l.at[a])

    def store_o(i):
        ready[0, i] = scatter_2(i, 0).total(u[i, 0, x].astype(F32)).astype(BF16)
        keep(i, 0).start()

    def store_x(i):
        ready[1, i] = scatter_2(i, 1).total(u[i, 1, y].astype(F32)).astype(BF16)
        keep(i, 1).start()

    def turn_in_relay(i):
        @pl.when(i == 0)
        def _():
            turn_in.forward()

    def turn_out_relay(i):
        @pl.when(i == chunks - 1)
        def _():
            turn_out.forward()

    plan = [
        (17, multiply_o),
        (17, multiply_x),
        (11, sum_z_g_relay),
        (14, gather_z_relay),
        (24, multiply_v),
        (1, gather_1x),
        (25, sum_2o),
        (16, multiply_w),
        (19, sum_1o_relay),
        (12, activate),
        (9, multiply_p),
        (24, sum_2x),
        (9, multiply_g),
        (41, store_o),
        (19, sum_1x_relay),
        (20, turn_out_relay),
        (6, gather_2x),
        (9, sum_z_p),
        (9, sum_z_g),
        (37, store_x),
        (15, gather_z),
        (1, gather_1c),
        (10, sum_z_p_relay),
        (6, gather_2c),
        (6, turn_in_relay),
    ]

    turn_in.start()

    def tick(now, _):
        for offset, stage in plan:
            i = now - offset

            @pl.when((i >= 0) & (i < chunks))
            def _():
                stage(i)

        return 0

    lax.fori_loop(0, chunks + max(offset for offset, _ in plan), tick, 0)

    keep_w = pltpu.make_async_copy(gw2, gw2_ref, s_l.at[3])
    gw2[...] = acc[1].astype(BF16)
    keep_w.start()

    def sent(blocks, semaphore):
        copy(blocks, blocks, semaphore, r_t.at[0], partner).wait_send()

    most = 3 * chunks // 4
    for a, all_blocks in ((0, ax), (1, ac)):
        sent(all_blocks.at[pl.ds(0, most), 0], s_g.at[0, a])
        sent(all_blocks.at[pl.ds(0, most)], s_g.at[1, a])
        sent(kr.at[:, a], s_k.at[a])
        sent(zr.at[:, a], s_z.at[a])
        sent(r1.at[:, a], s_o.at[0, a])
        sent(r2.at[:, a], s_o.at[1, a])
    sent(hg.at[pl.ds(0, most), :, 0], s_h.at[0])
    sent(hg.at[:, 0], s_p.at[0])
    turn_in.wait_send()
    turn_out.wait_recv()
    turn_out.wait_send()
    for a in (0, 1):
        pltpu.make_async_copy(ready.at[a], (out_ref, gx_ref)[a], r_l.at[a]).wait()
    keep_w.wait()


def fused(tokens, cotangent, weight_in, weight_out):
    dma = pltpu.SemaphoreType.DMA
    anywhere = pl.BlockSpec(memory_space=pl.ANY)
    return pl.pallas_call(
        kernel,
        out_shape=(
            jax.ShapeDtypeStruct((chunks, m, W), BF16),
            jax.ShapeDtypeStruct((chunks, m, W), BF16),
            jax.ShapeDtypeStruct((256, 2 * W), BF16),
            jax.ShapeDtypeStruct((W, W), BF16),
        ),
        in_specs=[anywhere] * 4,
        out_specs=(anywhere,) * 4,
        scratch_shapes=[
            pltpu.VMEM((chunks, 4, 4, m, W), BF16),
            pltpu.VMEM((chunks, 4, 4, m, W), BF16),
            pltpu.VMEM((chunks, 2, 2, 4, tz, W), F32),
            pltpu.VMEM((chunks, 2, 4, tz, W), F32),
            pltpu.VMEM((chunks, 2, 4, tz, W), BF16),
            pltpu.VMEM((chunks, 2, tz, W), BF16),
            pltpu.VMEM((chunks, 2, 3, tz, W), BF16),
            pltpu.VMEM((chunks, 2, 2, 4, tz, W), BF16),
            pltpu.VMEM((chunks, 4, 4, m, W), BF16),
            pltpu.VMEM((chunks, 4, 4, m, W), BF16),
            pltpu.VMEM((chunks, 2, 4, m, W), BF16),
            pltpu.VMEM((chunks, 2, 3, 4, m, W), BF16),
            pltpu.VMEM((chunks, 2, 4, m, W), BF16),
            pltpu.VMEM((chunks, 2, m, W), BF16),
            pltpu.VMEM((chunks, 2, 3, m, W), BF16),
            pltpu.VMEM((2, W, W), F32),
            pltpu.VMEM((2, 256, W), BF16),
            pltpu.VMEM((W, W), BF16),
            pltpu.VMEM((2, 256, W), BF16),
            pltpu.VMEM((W, W), BF16),
            pltpu.VMEM((2, 256, W), BF16),
            pltpu.VMEM((2, 256, W), BF16),
            pltpu.VMEM((2, chunks, m, W), BF16),
            dma((2, 2)), dma((chunks, 2, 2, 1 + max(relay_gather_1, relay_gather_2))),
            dma((2,)), dma((chunks, 2)),
            dma((2,)), dma((chunks, 2, 2)),
            dma((1,)), dma((chunks, 2)),
            dma((1,)), dma((chunks,)),
            dma((2, 2)), dma((chunks, 2, 2)), dma((chunks, 2)),
            dma((2, 2, 2)), dma((2, 2, pieces)), dma((2,)),
            dma((4,)), dma((2,)),
        ],
        compiler_params=pltpu.CompilerParams(
            collective_id=0, has_side_effects=True, vmem_limit_bytes=56 << 20
        ),
        cost_estimate=pl.CostEstimate(
            flops=6 * 2 * 2048 * W * W, bytes_accessed=3 << 20, transcendentals=2048 * W
        ),
    )(tokens.reshape(chunks, m, W), cotangent.reshape(chunks, m, W), weight_in, weight_out)


def hand_over(*refs):
    held, given, rooms, arrived, done = refs[:4], refs[4:8], refs[8:12], refs[12], refs[13]
    ways = []
    for i in range(4):
        rows = held[i].shape[0] // parts_of_result
        for j in range(parts_of_result):
            part = pl.ds(j * rows, rows)
            room = rooms[i].at[part]
            ways.append((
                pltpu.make_async_copy(held[i].at[part], room, arrived.at[i, j]),
                pltpu.make_async_copy(room, given[i].at[part], done.at[i, j]),
            ))
    for come, _ in ways:
        come.start()
    for come, go in ways:
        come.wait()
        go.start()
    for _, go in ways:
        go.wait()


def on_device(tokens, weight_in, weight_out, cotangent):
    output, grad_tokens, grad_in, grad_out = fused(tokens, cotangent, weight_in, weight_out)
    results = (output.reshape(128, W), grad_tokens.reshape(128, W), grad_in, grad_out)
    anywhere = pl.BlockSpec(memory_space=pl.ANY)
    return pl.pallas_call(
        hand_over,
        out_shape=[jax.ShapeDtypeStruct(r.shape, r.dtype) for r in results],
        in_specs=[anywhere] * 4,
        out_specs=[anywhere] * 4,
        scratch_shapes=[pltpu.VMEM(r.shape, r.dtype) for r in results]
        + [pltpu.SemaphoreType.DMA((4, parts_of_result))] * 2,
    )(*results)


def solution(mesh):
    placed = (P("row", "col"),) * 4
    return jax.shard_map(
        on_device, mesh=mesh, in_specs=placed, out_specs=placed, check_vma=False
    )
```

```python
import functools
import math

import jax
import jax.numpy as jnp
from jax import lax
from jax.experimental import pallas as pl
from jax.experimental.pallas import tpu as pltpu
from jax.sharding import PartitionSpec as P

MESH = pl.DeviceIdType.MESH
BF16 = jnp.bfloat16
F32 = jnp.float32

gelu_scale = math.sqrt(2.0 / math.pi)
cubic_term = 0.044715

chunks = 8
m = 128 // chunks
n = 16 * m
tz = n // 8
W = 512
parts_of_result = 2
pieces = 8

relay_gather_1, relay_gather_2 = False, False
relay_sum_z, relay_gather_z = True, True
relay_sum_1, relay_sum_2 = True, False


def activate_both(preact):
    square = preact * preact
    tanh_value = jnp.tanh(gelu_scale * (preact + cubic_term * square * preact))
    half = 0.5 * (1.0 + tanh_value)
    slope = half + 0.5 * preact * (1.0 - tanh_value * tanh_value) * gelu_scale * (
        1.0 + 3.0 * cubic_term * square
    )
    return preact * half, slope


def dot_nn(left, right):
    return jnp.dot(left, right, preferred_element_type=F32)


def dot_nt(left, right):
    return lax.dot_general(
        left, right, (((1,), (1,)), ((), ())), preferred_element_type=F32
    )


def dot_tn(left, right):
    return lax.dot_general(
        left, right, (((0,), (0,)), ((), ())), preferred_element_type=F32
    )


def kernel(
    x_ref, c_ref, win_ref, wout_ref,
    out_ref, gx_ref, gw1_ref, gw2_ref,
    ax, ac, part, kr, zs, zt, zr, hg, os, gs, t1, r1, u, t2, r2, acc,
    w1, w2, gw1, gw2, stay, back, ready, whole, kept,
    s_g, r_g, s_k, r_k, s_z, r_z, s_h, r_h, s_p, r_p, s_o, r_o, r_q, s_w, r_w, r_t, s_l, r_l,
):
    row, col = lax.axis_index("row"), lax.axis_index("col")
    x, y, z, k = row // 4, lax.rem(row, 4), col // 2, lax.rem(col, 2)
    sign = 1 - 2 * k

    rings = {
        id(here): [lax.rem(here + step * sign + 4, 4) for step in (0, 1, 2, -1)]
        for here in (x, y, z)
    }

    def at(here, step):
        return rings[id(here)][step % 4]

    def on_x(p):
        return (p * 4 + y, col)

    def on_y(p):
        return (x * 4 + p, col)

    def on_z(p):
        return (row, p * 2 + k)

    partner = (row, z * 2 + 1 - k)

    def copy(src, dst, send, recv, device):
        return pltpu.make_async_remote_copy(
            src_ref=src, dst_ref=dst, send_sem=send, recv_sem=recv,
            device_id=device, device_id_type=MESH,
        )

    def shift(b):
        return lax.rem(b + x + y, 4)

    def turn_target(b):
        return (lax.rem(z - shift(b) + 4, 4) * 4 + b, x * 2 + y // 2)

    def turn_source(slot):
        return (z * 4 + 2 * k + slot, lax.rem(x + y + z + 2 * k + slot, 4) * 2 + y // 2)

    home = (x == z) & (lax.rem(x + 2 * y, 4) == 0) & (k == y // 2)

    def is_home(j):
        return home & (lax.rem(y, 2) == j)

    barrier = pltpu.get_barrier_semaphore()

    def greet(device):
        pl.semaphore_signal(barrier, inc=1, device_id=device, device_id_type=MESH)

    for j in (1, 2, 3):
        greet(on_x(lax.rem(x + j, 4)))
        greet(on_y(lax.rem(y + j, 4)))
        greet(on_z(lax.rem(z + j, 4)))
    greet(partner)
    for j in (0, 1):

        @pl.when(jnp.logical_not(is_home(j)))
        def _():
            greet(turn_target(2 * k + j))
            greet(turn_source(j))

    loads = [
        pltpu.make_async_copy(x_ref, ax.at[:, x, y], s_l.at[0]),
        pltpu.make_async_copy(c_ref, ac.at[:, x, y], s_l.at[1]),
        pltpu.make_async_copy(wout_ref, w2, s_l.at[2]),
    ]
    for one in loads:
        one.start()
    acc[...] = jnp.zeros_like(acc)
    loads[0].wait()
    loads[1].wait()
    pl.semaphore_wait(barrier, 14 - 2 * home.astype(jnp.int32))

    size = 256 // pieces

    class Turn:
        def __init__(self, way, source, middle, target):
            self.way, self.source, self.middle, self.target = way, source, middle, target

        def move_1(self, j, q):
            where = (self.way, j, q)
            rows = pl.ds(q * size, size)
            return copy(
                self.source(j, rows), self.middle.at[j, rows], s_w.at[self.way, 0, j], r_w.at[where],
                on_z(lax.rem(z + shift(2 * k + j), 4)),
            )

        def move_2(self, j, q, slot):
            rows = pl.ds(q * size, size)
            return copy(
                self.middle.at[j, rows], self.target(slot, rows),
                s_w.at[self.way, 1, j], r_t.at[self.way], turn_target(2 * k + j),
            )

        def stay_1(self, j, q):
            rows = pl.ds(q * size, size)
            return pltpu.make_async_copy(
                self.source(j, rows), self.middle.at[j, rows], r_w.at[self.way, j, q]
            )

        def stay_2(self, j, q):
            rows = pl.ds(q * size, size)
            return pltpu.make_async_copy(
                self.middle.at[j, rows], self.target(j, rows), r_t.at[self.way]
            )

        def either(self, condition, yes, no):
            pl.when(condition)(yes)
            pl.when(jnp.logical_not(condition))(no)

        def start(self):
            for q in range(pieces):
                for j in (0, 1):
                    self.either(
                        shift(2 * k + j) == 0,
                        lambda: self.stay_1(j, q).start(),
                        lambda: self.move_1(j, q).start(),
                    )

        def forward(self):
            slot = lax.rem(y, 2)
            for q in range(pieces):
                for j in (0, 1):
                    self.move_1(j, q).wait_recv()
                    self.either(
                        is_home(j),
                        lambda: self.stay_2(j, q).start(),
                        lambda: self.move_2(j, q, slot).start(),
                    )

        def whole(self, j, stage):
            return copy(
                self.middle.at[j], self.middle.at[j], s_w.at[self.way, stage, j],
                r_t.at[self.way], partner,
            )

        def wait_recv(self):
            copy(
                self.middle, self.middle, s_w.at[self.way, 0, 0], r_t.at[self.way], partner
            ).wait_recv()

        def wait_send(self):
            for j in (0, 1):
                pl.when(shift(2 * k + j) != 0)(lambda: self.whole(j, 0).wait_send())
                pl.when(jnp.logical_not(is_home(j)))(lambda: self.whole(j, 1).wait_send())

    def half(slot):
        return pl.ds(pl.multiple_of(slot * W, W), W)

    turn_in = Turn(
        0, lambda j, rows: win_ref.at[rows, half(j)], stay, lambda slot, rows: w1.at[slot, rows]
    )
    turn_out = Turn(
        1, lambda j, rows: gw1.at[j, rows], back, lambda slot, rows: gw1_ref.at[rows, half(slot)]
    )

    class Gather:
        def __init__(self, relay, region, place, here, send, recvs):
            self.relay, self.region, self.place, self.here = relay, region, place, here
            self.send, self.recvs = send, recvs

        def move(self, p, step, to):
            first = self.relay and step == 1
            return copy(
                self.region(p), self.region(p), self.send, self.recvs.at[1 if first else 0],
                self.place(at(self.here, to)),
            )

        def start(self):
            if not self.relay:
                self.move(self.here, 2, 2).start()
            self.move(self.here, 1, 1).start()
            self.move(self.here, 3, -1).start()

        def forward(self):
            if self.relay:
                behind = at(self.here, -1)
                self.move(behind, 1, 1).wait_recv()
                self.move(behind, 2, 1).start()

        def wait_recv(self):
            blocks = self.region(pl.ds(0, 2 if self.relay else 3))
            copy(blocks, blocks, self.send, self.recvs.at[0], partner).wait_recv()

    class Scatter:
        def __init__(self, relay, source, held, got, place, here, send, recvs):
            self.relay, self.source, self.held, self.got = relay, source, held, got
            self.place, self.here, self.send, self.recvs = place, here, send, recvs

        def move(self, src, step, to):
            slot = {2: 0, 3: 1, 1: 2}[step]
            first = self.relay and step == 2
            return copy(
                src, self.got.at[slot], self.send, self.recvs.at[1 if first else 0],
                self.place(at(self.here, to)),
            )

        def start(self):
            self.move(self.source(at(self.here, 2)), 2, 1 if self.relay else 2).start()
            self.move(self.source(at(self.here, -1)), 3, -1).start()
            if not self.relay:
                self.move(self.source(at(self.here, 1)), 1, 1).start()

        def forward(self, own):
            if self.relay:
                self.move(self.source(self.here), 2, 1).wait_recv()
                self.held[...] = (own + self.got[0].astype(F32)).astype(BF16)
                self.move(self.held, 1, 1).start()

        def total(self, own):
            blocks = self.got.at[pl.ds(1, 2)] if self.relay else self.got
            copy(blocks, blocks, self.send, self.recvs.at[0], partner).wait_recv()
            for slot in (1, 2) if self.relay else (0, 1, 2):
                own = own + self.got[slot].astype(F32)
            return own

    def gather_x(i, phase):
        region = (lambda p: ax.at[i, p, y]) if phase == 0 else (lambda p: ax.at[i, :, p])
        place, here = ((on_x, x), (on_y, y))[phase]
        relay = (relay_gather_1, relay_gather_2)[phase]
        return Gather(relay, region, place, here, s_g.at[phase, 0], r_g.at[i, phase, 0])

    def gather_c(i, phase):
        region = (lambda p: ac.at[i, x, p]) if phase == 0 else (lambda p: ac.at[i, p])
        place, here = ((on_y, y), (on_x, x))[phase]
        relay = (relay_gather_1, relay_gather_2)[phase]
        return Gather(relay, region, place, here, s_g.at[phase, 1], r_g.at[i, phase, 1])

    def gather_h(i):
        return Gather(
            relay_gather_z, lambda p: hg.at[i, :, k, p], on_z, z, s_h.at[0], r_h.at[i]
        )

    def exchange(i, w):
        return copy(part.at[i, w, 1 - k], kr.at[i, w], s_k.at[w], r_k.at[i, w], partner)

    def scatter_z(i, w):
        return Scatter(
            relay_sum_z, lambda p: zs.at[i, w, p], zt.at[i, w], zr.at[i, w], on_z, z,
            s_z.at[w], r_z.at[i, w],
        )

    def pair(i, p):
        return copy(
            hg.at[i, :, k, p], hg.at[i, :, k, p], s_p.at[0], r_p.at[i], partner
        )

    def scatter_1(i, a):
        source = (lambda p: os.at[i, :, p]) if a == 0 else (lambda p: gs.at[i, p])
        place, here = ((on_y, y), (on_x, x))[a]
        return Scatter(
            relay_sum_1, source, t1.at[i, a], r1.at[i, a], place, here,
            s_o.at[0, a], r_o.at[i, a],
        )

    def scatter_2(i, a):
        place, here = ((on_x, x), (on_y, y))[a]
        return Scatter(
            relay_sum_2, lambda p: u.at[i, a, p], t2.at[i, a], r2.at[i, a], place, here,
            s_o.at[1, a], r_q.at[i, pl.ds(a, 1)],
        )

    def gather_1x(i):
        gather_x(i, 0).start()

    def gather_1c(i):
        gather_c(i, 0).start()

    def gather_2x(i):
        gather_x(i, 0).wait_recv()
        gather_x(i, 1).start()

    def gather_2c(i):
        gather_c(i, 0).wait_recv()
        gather_c(i, 1).start()

    def gather_2x_relay(i):
        gather_x(i, 1).forward()

    def gather_2c_relay(i):
        gather_c(i, 1).forward()

    def give(i, w, product):
        part[i, w] = product.reshape(2, 4, tz, W)
        exchange(i, w).start()

    def mixed(i, w, p):
        return part[i, w, k, p] + kr[i, w, p]

    def multiply_g(i):
        @pl.when(i == 0)
        def _():
            loads[2].wait()

        gather_c(i, 1).wait_recv()
        give(i, 1, dot_nt(ac[i].reshape(n, W), w2[...]))

    def multiply_p(i):
        @pl.when(i == 0)
        def _():
            turn_in.wait_recv()

        gather_x(i, 1).wait_recv()
        give(i, 0, dot_nn(ax[i].reshape(n, W), w1[...].reshape(W, W)))

    def sum_z(i, w):
        exchange(i, w).wait_recv()
        for p in range(4):
            zs[i, w, p] = mixed(i, w, p).astype(BF16)
        scatter_z(i, w).start()

    def sum_z_p(i):
        sum_z(i, 0)

    def sum_z_g(i):
        sum_z(i, 1)

    def sum_z_p_relay(i):
        scatter_z(i, 0).forward(mixed(i, 0, at(z, 1)))

    def sum_z_g_relay(i):
        scatter_z(i, 1).forward(mixed(i, 1, at(z, 1)))

    def activate(i):
        grad = scatter_z(i, 1).total(mixed(i, 1, z))
        hidden, slope = activate_both(scatter_z(i, 0).total(mixed(i, 0, z)))
        hg[i, 0, k, z] = hidden.astype(BF16)
        hg[i, 1, k, z] = (grad * slope).astype(BF16)
        gather_h(i).start()
        pair(i, z).start()

    def gather_z_relay(i):
        gather_h(i).forward()
        if relay_gather_z:
            pair(i, at(z, -1)).start()

    def gather_z(i):
        gather_h(i).wait_recv()
        if not relay_gather_z:
            pair(i, at(z, -1)).start()
        pair(i, at(z, 1)).start()
        pair(i, at(z, 2)).start()

    def multiply_w(i):
        others = hg.at[i, :, 1 - k]
        copy(others, others, s_p.at[0], r_p.at[i], partner).wait_recv()
        acc[0] += dot_tn(ax[i].reshape(n, W), hg[i, 1].reshape(n, W))

        @pl.when(i == chunks - 1)
        def _():
            gw1[...] = acc[0].astype(BF16).reshape(2, 256, W)
            turn_out.start()

    def multiply_o(i):
        product = dot_nn(hg[i, 0].reshape(n, W), w2[...])
        whole[i, 0] = product.reshape(4, 4, m, W)
        os[i] = product.astype(BF16).reshape(4, 4, m, W)
        scatter_1(i, 0).start()

    def multiply_x(i):
        product = dot_nt(hg[i, 1].reshape(n, W), w1[...].reshape(W, W))
        whole[i, 1] = product.reshape(4, 4, m, W)
        gs[i] = product.astype(BF16).reshape(4, 4, m, W)
        scatter_1(i, 1).start()

    def multiply_v(i):
        acc[1] += dot_tn(hg[i, 0].reshape(n, W), ac[i].reshape(n, W))

    def sum_1o_relay(i):
        scatter_1(i, 0).forward(whole[i, 0, :, at(y, 1)])

    def sum_1x_relay(i):
        scatter_1(i, 1).forward(whole[i, 1, at(x, 1)])

    def sum_2o(i):
        total = scatter_1(i, 0).total(whole[i, 0, :, y])
        kept[i, 0] = total
        u[i, 0] = total.astype(BF16)
        scatter_2(i, 0).start()

    def sum_2x(i):
        total = scatter_1(i, 1).total(whole[i, 1, x])
        kept[i, 1] = total
        u[i, 1] = total.astype(BF16)
        scatter_2(i, 1).start()

    def keep(i, a):
        return pltpu.make_async_copy(ready.at[a, i], (out_ref, gx_ref)[a].at[i], r_l.at[a])

    def store_o(i):
        ready[0, i] = scatter_2(i, 0).total(kept[i, 0, x]).astype(BF16)
        keep(i, 0).start()

    def store_x(i):
        ready[1, i] = scatter_2(i, 1).total(kept[i, 1, y]).astype(BF16)
        keep(i, 1).start()

    def turn_in_relay(i):
        @pl.when(i == 0)
        def _():
            turn_in.forward()

    def turn_out_relay(i):
        @pl.when(i == chunks - 1)
        def _():
            turn_out.forward()

    plan = [
        (17, multiply_o),
        (17, multiply_x),
        (11, sum_z_g_relay),
        (14, gather_z_relay),
        (24, multiply_v),
        (1, gather_1x),
        (25, sum_2o),
        (16, multiply_w),
        (19, sum_1o_relay),
        (12, activate),
        (9, multiply_p),
        (24, sum_2x),
        (9, multiply_g),
        (41, store_o),
        (19, sum_1x_relay),
        (20, turn_out_relay),
        (6, gather_2x),
        (9, sum_z_p),
        (9, sum_z_g),
        (37, store_x),
        (15, gather_z),
        (1, gather_1c),
        (10, sum_z_p_relay),
        (6, gather_2c),
        (6, turn_in_relay),
    ]

    turn_in.start()

    def tick(now, _):
        for offset, stage in plan:
            i = now - offset

            @pl.when((i >= 0) & (i < chunks))
            def _():
                stage(i)

        return 0

    lax.fori_loop(0, chunks + max(offset for offset, _ in plan), tick, 0)

    keep_w = pltpu.make_async_copy(gw2, gw2_ref, s_l.at[3])
    gw2[...] = acc[1].astype(BF16)
    keep_w.start()

    def sent(blocks, semaphore):
        copy(blocks, blocks, semaphore, r_t.at[0], partner).wait_send()

    most = 3 * chunks // 4
    for a, all_blocks in ((0, ax), (1, ac)):
        sent(all_blocks.at[pl.ds(0, most), 0], s_g.at[0, a])
        sent(all_blocks.at[pl.ds(0, most)], s_g.at[1, a])
        sent(kr.at[:, a], s_k.at[a])
        sent(zr.at[:, a], s_z.at[a])
        sent(r1.at[:, a], s_o.at[0, a])
        sent(r2.at[:, a], s_o.at[1, a])
    sent(hg.at[pl.ds(0, most), :, 0], s_h.at[0])
    sent(hg.at[:, 0], s_p.at[0])
    turn_in.wait_send()
    turn_out.wait_recv()
    turn_out.wait_send()
    for a in (0, 1):
        pltpu.make_async_copy(ready.at[a], (out_ref, gx_ref)[a], r_l.at[a]).wait()
    keep_w.wait()


def fused(tokens, cotangent, weight_in, weight_out):
    dma = pltpu.SemaphoreType.DMA
    anywhere = pl.BlockSpec(memory_space=pl.ANY)
    return pl.pallas_call(
        kernel,
        out_shape=(
            jax.ShapeDtypeStruct((chunks, m, W), BF16),
            jax.ShapeDtypeStruct((chunks, m, W), BF16),
            jax.ShapeDtypeStruct((256, 2 * W), BF16),
            jax.ShapeDtypeStruct((W, W), BF16),
        ),
        in_specs=[anywhere] * 4,
        out_specs=(anywhere,) * 4,
        scratch_shapes=[
            pltpu.VMEM((chunks, 4, 4, m, W), BF16),
            pltpu.VMEM((chunks, 4, 4, m, W), BF16),
            pltpu.VMEM((chunks, 2, 2, 4, tz, W), F32),
            pltpu.VMEM((chunks, 2, 4, tz, W), F32),
            pltpu.VMEM((chunks, 2, 4, tz, W), BF16),
            pltpu.VMEM((chunks, 2, tz, W), BF16),
            pltpu.VMEM((chunks, 2, 3, tz, W), BF16),
            pltpu.VMEM((chunks, 2, 2, 4, tz, W), BF16),
            pltpu.VMEM((chunks, 4, 4, m, W), BF16),
            pltpu.VMEM((chunks, 4, 4, m, W), BF16),
            pltpu.VMEM((chunks, 2, 4, m, W), BF16),
            pltpu.VMEM((chunks, 2, 3, 4, m, W), BF16),
            pltpu.VMEM((chunks, 2, 4, m, W), BF16),
            pltpu.VMEM((chunks, 2, m, W), BF16),
            pltpu.VMEM((chunks, 2, 3, m, W), BF16),
            pltpu.VMEM((2, W, W), F32),
            pltpu.VMEM((2, 256, W), BF16),
            pltpu.VMEM((W, W), BF16),
            pltpu.VMEM((2, 256, W), BF16),
            pltpu.VMEM((W, W), BF16),
            pltpu.VMEM((2, 256, W), BF16),
            pltpu.VMEM((2, 256, W), BF16),
            pltpu.VMEM((2, chunks, m, W), BF16),
            pltpu.VMEM((chunks, 2, 4, 4, m, W), F32),
            pltpu.VMEM((chunks, 2, 4, m, W), F32),
            dma((2, 2)), dma((chunks, 2, 2, 1 + max(relay_gather_1, relay_gather_2))),
            dma((2,)), dma((chunks, 2)),
            dma((2,)), dma((chunks, 2, 2)),
            dma((1,)), dma((chunks, 2)),
            dma((1,)), dma((chunks,)),
            dma((2, 2)), dma((chunks, 2, 2)), dma((chunks, 2)),
            dma((2, 2, 2)), dma((2, 2, pieces)), dma((2,)),
            dma((4,)), dma((2,)),
        ],
        compiler_params=pltpu.CompilerParams(
            collective_id=0, has_side_effects=True, vmem_limit_bytes=58 << 20
        ),
        cost_estimate=pl.CostEstimate(
            flops=6 * 2 * 2048 * W * W, bytes_accessed=3 << 20, transcendentals=2048 * W
        ),
    )(tokens.reshape(chunks, m, W), cotangent.reshape(chunks, m, W), weight_in, weight_out)


def hand_over(*refs):
    held, given, rooms, arrived, done = refs[:4], refs[4:8], refs[8:12], refs[12], refs[13]
    ways = []
    for i in range(4):
        rows = held[i].shape[0] // parts_of_result
        for j in range(parts_of_result):
            part = pl.ds(j * rows, rows)
            room = rooms[i].at[part]
            ways.append((
                pltpu.make_async_copy(held[i].at[part], room, arrived.at[i, j]),
                pltpu.make_async_copy(room, given[i].at[part], done.at[i, j]),
            ))
    for come, _ in ways:
        come.start()
    for come, go in ways:
        come.wait()
        go.start()
    for _, go in ways:
        go.wait()


def on_device(tokens, weight_in, weight_out, cotangent):
    output, grad_tokens, grad_in, grad_out = fused(tokens, cotangent, weight_in, weight_out)
    results = (output.reshape(128, W), grad_tokens.reshape(128, W), grad_in, grad_out)
    anywhere = pl.BlockSpec(memory_space=pl.ANY)
    return pl.pallas_call(
        hand_over,
        out_shape=[jax.ShapeDtypeStruct(r.shape, r.dtype) for r in results],
        in_specs=[anywhere] * 4,
        out_specs=[anywhere] * 4,
        scratch_shapes=[pltpu.VMEM(r.shape, r.dtype) for r in results]
        + [pltpu.SemaphoreType.DMA((4, parts_of_result))] * 2,
    )(*results)


def solution(mesh):
    placed = (P("row", "col"),) * 4
    return jax.shard_map(
        on_device, mesh=mesh, in_specs=placed, out_specs=placed, check_vma=False
    )
```

```python
import functools
import math

import jax
import jax.numpy as jnp
from jax import lax
from jax.experimental import pallas as pl
from jax.experimental.pallas import tpu as pltpu
from jax.sharding import PartitionSpec as P

MESH = pl.DeviceIdType.MESH
BF16 = jnp.bfloat16
F32 = jnp.float32

gelu_scale = math.sqrt(2.0 / math.pi)
cubic_term = 0.044715

chunks = 8
m = 128 // chunks
n = 16 * m
tz = n // 8
W = 512
parts_of_result = 2
pieces = 8

relay_gather_1, relay_gather_2 = False, False
relay_sum_z, relay_gather_z = True, True
relay_sum_1, relay_sum_2 = True, False


def activate_both(preact):
    square = preact * preact
    tanh_value = jnp.tanh(gelu_scale * (preact + cubic_term * square * preact))
    half = 0.5 * (1.0 + tanh_value)
    slope = half + 0.5 * preact * (1.0 - tanh_value * tanh_value) * gelu_scale * (
        1.0 + 3.0 * cubic_term * square
    )
    return preact * half, slope


def dot_nn(left, right):
    return jnp.dot(left, right, preferred_element_type=F32)


def dot_nt(left, right):
    return lax.dot_general(
        left, right, (((1,), (1,)), ((), ())), preferred_element_type=F32
    )


def dot_tn(left, right):
    return lax.dot_general(
        left, right, (((0,), (0,)), ((), ())), preferred_element_type=F32
    )


def kernel(
    x_ref, c_ref, win_ref, wout_ref,
    out_ref, gx_ref, gw1_ref, gw2_ref,
    ax, ac, part, kr, zs, zt, zr, hg, os, gs, t1, r1, u, t2, r2, acc,
    w1, w2, gw1, gw2, stay, back, ready, whole, kept,
    s_g, r_g, s_k, r_k, s_z, r_z, s_h, r_h, s_p, r_p, s_o, r_o, r_q, s_w, r_w, r_t, s_l, r_l,
):
    row, col = lax.axis_index("row"), lax.axis_index("col")
    x, y, z, k = row // 4, lax.rem(row, 4), col // 2, lax.rem(col, 2)
    sign = 1 - 2 * k

    rings = {
        id(here): [lax.rem(here + step * sign + 4, 4) for step in (0, 1, 2, -1)]
        for here in (x, y, z)
    }

    def at(here, step):
        return rings[id(here)][step % 4]

    def on_x(p):
        return (p * 4 + y, col)

    def on_y(p):
        return (x * 4 + p, col)

    def on_z(p):
        return (row, p * 2 + k)

    partner = (row, z * 2 + 1 - k)

    def copy(src, dst, send, recv, device):
        return pltpu.make_async_remote_copy(
            src_ref=src, dst_ref=dst, send_sem=send, recv_sem=recv,
            device_id=device, device_id_type=MESH,
        )

    def shift(b):
        return lax.rem(b + x + y, 4)

    def turn_target(b):
        return (lax.rem(z - shift(b) + 4, 4) * 4 + b, x * 2 + y // 2)

    def turn_source(slot):
        return (z * 4 + 2 * k + slot, lax.rem(x + y + z + 2 * k + slot, 4) * 2 + y // 2)

    home = (x == z) & (lax.rem(x + 2 * y, 4) == 0) & (k == y // 2)

    def is_home(j):
        return home & (lax.rem(y, 2) == j)

    barrier = pltpu.get_barrier_semaphore()

    def greet(device):
        pl.semaphore_signal(barrier, inc=1, device_id=device, device_id_type=MESH)

    for j in (1, 2, 3):
        greet(on_x(lax.rem(x + j, 4)))
        greet(on_y(lax.rem(y + j, 4)))
        greet(on_z(lax.rem(z + j, 4)))
    greet(partner)
    for j in (0, 1):

        @pl.when(jnp.logical_not(is_home(j)))
        def _():
            greet(turn_target(2 * k + j))
            greet(turn_source(j))

    loads = [
        pltpu.make_async_copy(x_ref, ax.at[:, x, y], s_l.at[0]),
        pltpu.make_async_copy(c_ref, ac.at[:, x, y], s_l.at[1]),
        pltpu.make_async_copy(wout_ref, w2, s_l.at[2]),
    ]
    for one in loads:
        one.start()
    acc[...] = jnp.zeros_like(acc)
    loads[0].wait()
    loads[1].wait()
    pl.semaphore_wait(barrier, 14 - 2 * home.astype(jnp.int32))

    size = 256 // pieces

    class Turn:
        def __init__(self, way, source, middle, target):
            self.way, self.source, self.middle, self.target = way, source, middle, target

        def move_1(self, j, q):
            where = (self.way, j, q)
            rows = pl.ds(q * size, size)
            return copy(
                self.source(j, rows), self.middle.at[j, rows], s_w.at[self.way, 0, j], r_w.at[where],
                on_z(lax.rem(z + shift(2 * k + j), 4)),
            )

        def move_2(self, j, q, slot):
            rows = pl.ds(q * size, size)
            return copy(
                self.middle.at[j, rows], self.target(slot, rows),
                s_w.at[self.way, 1, j], r_t.at[self.way], turn_target(2 * k + j),
            )

        def stay_1(self, j, q):
            rows = pl.ds(q * size, size)
            return pltpu.make_async_copy(
                self.source(j, rows), self.middle.at[j, rows], r_w.at[self.way, j, q]
            )

        def stay_2(self, j, q):
            rows = pl.ds(q * size, size)
            return pltpu.make_async_copy(
                self.middle.at[j, rows], self.target(j, rows), r_t.at[self.way]
            )

        def either(self, condition, yes, no):
            pl.when(condition)(yes)
            pl.when(jnp.logical_not(condition))(no)

        def start(self):
            for q in range(pieces):
                for j in (0, 1):
                    self.either(
                        shift(2 * k + j) == 0,
                        lambda: self.stay_1(j, q).start(),
                        lambda: self.move_1(j, q).start(),
                    )

        def forward(self):
            slot = lax.rem(y, 2)
            for q in range(pieces):
                for j in (0, 1):
                    self.move_1(j, q).wait_recv()
                    self.either(
                        is_home(j),
                        lambda: self.stay_2(j, q).start(),
                        lambda: self.move_2(j, q, slot).start(),
                    )

        def whole(self, j, stage):
            return copy(
                self.middle.at[j], self.middle.at[j], s_w.at[self.way, stage, j],
                r_t.at[self.way], partner,
            )

        def wait_recv(self):
            copy(
                self.middle, self.middle, s_w.at[self.way, 0, 0], r_t.at[self.way], partner
            ).wait_recv()

        def wait_send(self):
            for j in (0, 1):
                pl.when(shift(2 * k + j) != 0)(lambda: self.whole(j, 0).wait_send())
                pl.when(jnp.logical_not(is_home(j)))(lambda: self.whole(j, 1).wait_send())

    def half(slot):
        return pl.ds(pl.multiple_of(slot * W, W), W)

    turn_in = Turn(
        0, lambda j, rows: win_ref.at[rows, half(j)], stay, lambda slot, rows: w1.at[slot, rows]
    )
    turn_out = Turn(
        1, lambda j, rows: gw1.at[j, rows], back, lambda slot, rows: gw1_ref.at[rows, half(slot)]
    )

    class Gather:
        def __init__(self, relay, region, place, here, send, recvs):
            self.relay, self.region, self.place, self.here = relay, region, place, here
            self.send, self.recvs = send, recvs

        def move(self, p, step, to):
            first = self.relay and step == 1
            return copy(
                self.region(p), self.region(p), self.send, self.recvs.at[1 if first else 0],
                self.place(at(self.here, to)),
            )

        def start(self):
            if not self.relay:
                self.move(self.here, 2, 2).start()
            self.move(self.here, 1, 1).start()
            self.move(self.here, 3, -1).start()

        def forward(self):
            if self.relay:
                behind = at(self.here, -1)
                self.move(behind, 1, 1).wait_recv()
                self.move(behind, 2, 1).start()

        def wait_recv(self):
            blocks = self.region(pl.ds(0, 2 if self.relay else 3))
            copy(blocks, blocks, self.send, self.recvs.at[0], partner).wait_recv()

    class Scatter:
        def __init__(self, relay, source, held, got, place, here, send, recvs):
            self.relay, self.source, self.held, self.got = relay, source, held, got
            self.place, self.here, self.send, self.recvs = place, here, send, recvs

        def move(self, src, step, to):
            slot = {2: 0, 3: 1, 1: 2}[step]
            first = self.relay and step == 2
            return copy(
                src, self.got.at[slot], self.send, self.recvs.at[1 if first else 0],
                self.place(at(self.here, to)),
            )

        def start(self):
            self.move(self.source(at(self.here, 2)), 2, 1 if self.relay else 2).start()
            self.move(self.source(at(self.here, -1)), 3, -1).start()
            if not self.relay:
                self.move(self.source(at(self.here, 1)), 1, 1).start()

        def forward(self, own):
            if self.relay:
                self.move(self.source(self.here), 2, 1).wait_recv()
                self.held[...] = (own + self.got[0].astype(F32)).astype(BF16)
                self.move(self.held, 1, 1).start()

        def total(self, own):
            blocks = self.got.at[pl.ds(1, 2)] if self.relay else self.got
            copy(blocks, blocks, self.send, self.recvs.at[0], partner).wait_recv()
            for slot in (1, 2) if self.relay else (0, 1, 2):
                own = own + self.got[slot].astype(F32)
            return own

    def gather_x(i, phase):
        region = (lambda p: ax.at[i, p, y]) if phase == 0 else (lambda p: ax.at[i, :, p])
        place, here = ((on_x, x), (on_y, y))[phase]
        relay = (relay_gather_1, relay_gather_2)[phase]
        return Gather(relay, region, place, here, s_g.at[phase, 0], r_g.at[i, phase, 0])

    def gather_c(i, phase):
        region = (lambda p: ac.at[i, x, p]) if phase == 0 else (lambda p: ac.at[i, p])
        place, here = ((on_y, y), (on_x, x))[phase]
        relay = (relay_gather_1, relay_gather_2)[phase]
        return Gather(relay, region, place, here, s_g.at[phase, 1], r_g.at[i, phase, 1])

    def gather_h(i):
        return Gather(
            relay_gather_z, lambda p: hg.at[i, :, k, p], on_z, z, s_h.at[0], r_h.at[i]
        )

    def exchange(i, w):
        return copy(part.at[i, w, 1 - k], kr.at[i, w], s_k.at[w], r_k.at[i, w], partner)

    def scatter_z(i, w):
        return Scatter(
            relay_sum_z, lambda p: zs.at[i, w, p], zt.at[i, w], zr.at[i, w], on_z, z,
            s_z.at[w], r_z.at[i, w],
        )

    def pair(i, p):
        return copy(
            hg.at[i, :, k, p], hg.at[i, :, k, p], s_p.at[0], r_p.at[i], partner
        )

    def scatter_1(i, a):
        source = (lambda p: os.at[i, :, p]) if a == 0 else (lambda p: gs.at[i, p])
        place, here = ((on_y, y), (on_x, x))[a]
        return Scatter(
            relay_sum_1, source, t1.at[i, a], r1.at[i, a], place, here,
            s_o.at[0, a], r_o.at[i, a],
        )

    def scatter_2(i, a):
        place, here = ((on_x, x), (on_y, y))[a]
        return Scatter(
            relay_sum_2, lambda p: u.at[i, a, p], t2.at[i, a], r2.at[i, a], place, here,
            s_o.at[1, a], r_q.at[i, pl.ds(a, 1)],
        )

    def gather_1x(i):
        gather_x(i, 0).start()

    def gather_1c(i):
        gather_c(i, 0).start()

    def gather_2x(i):
        gather_x(i, 0).wait_recv()
        gather_x(i, 1).start()

    def gather_2c(i):
        gather_c(i, 0).wait_recv()
        gather_c(i, 1).start()

    def gather_2x_relay(i):
        gather_x(i, 1).forward()

    def gather_2c_relay(i):
        gather_c(i, 1).forward()

    def give(i, w, product):
        part[i, w] = product.reshape(2, 4, tz, W)
        exchange(i, w).start()

    def mixed(i, w, p):
        return part[i, w, k, p] + kr[i, w, p]

    def multiply_g(i):
        @pl.when(i == 0)
        def _():
            loads[2].wait()

        gather_c(i, 1).wait_recv()
        give(i, 1, dot_nt(ac[i].reshape(n, W), w2[...]))

    def multiply_p(i):
        @pl.when(i == 0)
        def _():
            turn_in.wait_recv()

        gather_x(i, 1).wait_recv()
        give(i, 0, dot_nn(ax[i].reshape(n, W), w1[...].reshape(W, W)))

    def sum_z(i, w):
        exchange(i, w).wait_recv()
        for p in range(4):
            zs[i, w, p] = mixed(i, w, p).astype(BF16)
        scatter_z(i, w).start()

    def sum_z_p(i):
        sum_z(i, 0)

    def sum_z_g(i):
        sum_z(i, 1)

    def sum_z_p_relay(i):
        scatter_z(i, 0).forward(mixed(i, 0, at(z, 1)))

    def sum_z_g_relay(i):
        scatter_z(i, 1).forward(mixed(i, 1, at(z, 1)))

    def activate(i):
        grad = scatter_z(i, 1).total(mixed(i, 1, z))
        hidden, slope = activate_both(scatter_z(i, 0).total(mixed(i, 0, z)))
        hg[i, 0, k, z] = hidden.astype(BF16)
        hg[i, 1, k, z] = (grad * slope).astype(BF16)
        gather_h(i).start()
        pair(i, z).start()

    def gather_z_relay(i):
        gather_h(i).forward()
        if relay_gather_z:
            pair(i, at(z, -1)).start()

    def gather_z(i):
        gather_h(i).wait_recv()
        if not relay_gather_z:
            pair(i, at(z, -1)).start()
        pair(i, at(z, 1)).start()
        pair(i, at(z, 2)).start()

    def multiply_w(i):
        others = hg.at[i, :, 1 - k]
        copy(others, others, s_p.at[0], r_p.at[i], partner).wait_recv()
        acc[0] += dot_tn(ax[i].reshape(n, W), hg[i, 1].reshape(n, W))

        @pl.when(i == chunks - 1)
        def _():
            gw1[...] = acc[0].astype(BF16).reshape(2, 256, W)
            turn_out.start()

    def multiply_o(i):
        product = dot_nn(hg[i, 0].reshape(n, W), w2[...])
        whole[i, 0] = product.reshape(4, 4, m, W)
        os[i] = product.astype(BF16).reshape(4, 4, m, W)
        scatter_1(i, 0).start()

    def multiply_x(i):
        product = dot_nt(hg[i, 1].reshape(n, W), w1[...].reshape(W, W))
        whole[i, 1] = product.reshape(4, 4, m, W)
        gs[i] = product.astype(BF16).reshape(4, 4, m, W)
        scatter_1(i, 1).start()

    def multiply_v(i):
        acc[1] += dot_tn(hg[i, 0].reshape(n, W), ac[i].reshape(n, W))

    def sum_1o_relay(i):
        scatter_1(i, 0).forward(whole[i, 0, :, at(y, 1)])

    def sum_1x_relay(i):
        scatter_1(i, 1).forward(whole[i, 1, at(x, 1)])

    def sum_2o(i):
        total = scatter_1(i, 0).total(whole[i, 0, :, y])
        kept[i, 0] = total
        u[i, 0] = total.astype(BF16)
        scatter_2(i, 0).start()

    def sum_2x(i):
        total = scatter_1(i, 1).total(whole[i, 1, x])
        kept[i, 1] = total
        u[i, 1] = total.astype(BF16)
        scatter_2(i, 1).start()

    def keep(i, a):
        return pltpu.make_async_copy(ready.at[a, i], (out_ref, gx_ref)[a].at[i], r_l.at[a])

    def store_o(i):
        ready[0, i] = scatter_2(i, 0).total(kept[i, 0, x]).astype(BF16)
        keep(i, 0).start()

    def store_x(i):
        ready[1, i] = scatter_2(i, 1).total(kept[i, 1, y]).astype(BF16)
        keep(i, 1).start()

    def turn_in_relay(i):
        @pl.when(i == 0)
        def _():
            turn_in.forward()

    def turn_out_relay(i):
        @pl.when(i == chunks - 1)
        def _():
            turn_out.forward()

    plan = [
        (17, multiply_o),
        (17, multiply_x),
        (11, sum_z_g_relay),
        (14, gather_z_relay),
        (24, multiply_v),
        (1, gather_1x),
        (25, sum_2o),
        (16, multiply_w),
        (19, sum_1o_relay),
        (12, activate),
        (9, multiply_p),
        (24, sum_2x),
        (9, multiply_g),
        (31, store_o),
        (19, sum_1x_relay),
        (20, turn_out_relay),
        (6, gather_2x),
        (9, sum_z_p),
        (9, sum_z_g),
        (30, store_x),
        (15, gather_z),
        (1, gather_1c),
        (10, sum_z_p_relay),
        (6, gather_2c),
        (6, turn_in_relay),
    ]

    turn_in.start()

    def tick(now, _):
        for offset, stage in plan:
            i = now - offset

            @pl.when((i >= 0) & (i < chunks))
            def _():
                stage(i)

        return 0

    lax.fori_loop(0, chunks + max(offset for offset, _ in plan), tick, 0)

    keep_w = pltpu.make_async_copy(gw2, gw2_ref, s_l.at[3])
    gw2[...] = acc[1].astype(BF16)
    keep_w.start()

    def sent(blocks, semaphore):
        copy(blocks, blocks, semaphore, r_t.at[0], partner).wait_send()

    most = 3 * chunks // 4
    for a, all_blocks in ((0, ax), (1, ac)):
        sent(all_blocks.at[pl.ds(0, most), 0], s_g.at[0, a])
        sent(all_blocks.at[pl.ds(0, most)], s_g.at[1, a])
        sent(kr.at[:, a], s_k.at[a])
        sent(zr.at[:, a], s_z.at[a])
        sent(r1.at[:, a], s_o.at[0, a])
        sent(r2.at[:, a], s_o.at[1, a])
    sent(hg.at[pl.ds(0, most), :, 0], s_h.at[0])
    sent(hg.at[:, 0], s_p.at[0])
    turn_in.wait_send()
    turn_out.wait_recv()
    turn_out.wait_send()
    for a in (0, 1):
        pltpu.make_async_copy(ready.at[a], (out_ref, gx_ref)[a], r_l.at[a]).wait()
    keep_w.wait()


def fused(tokens, cotangent, weight_in, weight_out):
    dma = pltpu.SemaphoreType.DMA
    anywhere = pl.BlockSpec(memory_space=pl.ANY)
    return pl.pallas_call(
        kernel,
        out_shape=(
            jax.ShapeDtypeStruct((chunks, m, W), BF16),
            jax.ShapeDtypeStruct((chunks, m, W), BF16),
            jax.ShapeDtypeStruct((256, 2 * W), BF16),
            jax.ShapeDtypeStruct((W, W), BF16),
        ),
        in_specs=[anywhere] * 4,
        out_specs=(anywhere,) * 4,
        scratch_shapes=[
            pltpu.VMEM((chunks, 4, 4, m, W), BF16),
            pltpu.VMEM((chunks, 4, 4, m, W), BF16),
            pltpu.VMEM((chunks, 2, 2, 4, tz, W), F32),
            pltpu.VMEM((chunks, 2, 4, tz, W), F32),
            pltpu.VMEM((chunks, 2, 4, tz, W), BF16),
            pltpu.VMEM((chunks, 2, tz, W), BF16),
            pltpu.VMEM((chunks, 2, 3, tz, W), BF16),
            pltpu.VMEM((chunks, 2, 2, 4, tz, W), BF16),
            pltpu.VMEM((chunks, 4, 4, m, W), BF16),
            pltpu.VMEM((chunks, 4, 4, m, W), BF16),
            pltpu.VMEM((chunks, 2, 4, m, W), BF16),
            pltpu.VMEM((chunks, 2, 3, 4, m, W), BF16),
            pltpu.VMEM((chunks, 2, 4, m, W), BF16),
            pltpu.VMEM((chunks, 2, m, W), BF16),
            pltpu.VMEM((chunks, 2, 3, m, W), BF16),
            pltpu.VMEM((2, W, W), F32),
            pltpu.VMEM((2, 256, W), BF16),
            pltpu.VMEM((W, W), BF16),
            pltpu.VMEM((2, 256, W), BF16),
            pltpu.VMEM((W, W), BF16),
            pltpu.VMEM((2, 256, W), BF16),
            pltpu.VMEM((2, 256, W), BF16),
            pltpu.VMEM((2, chunks, m, W), BF16),
            pltpu.VMEM((chunks, 2, 4, 4, m, W), F32),
            pltpu.VMEM((chunks, 2, 4, m, W), F32),
            dma((2, 2)), dma((chunks, 2, 2, 1 + max(relay_gather_1, relay_gather_2))),
            dma((2,)), dma((chunks, 2)),
            dma((2,)), dma((chunks, 2, 2)),
            dma((1,)), dma((chunks, 2)),
            dma((1,)), dma((chunks,)),
            dma((2, 2)), dma((chunks, 2, 2)), dma((chunks, 2)),
            dma((2, 2, 2)), dma((2, 2, pieces)), dma((2,)),
            dma((4,)), dma((2,)),
        ],
        compiler_params=pltpu.CompilerParams(
            collective_id=0, has_side_effects=True, vmem_limit_bytes=58 << 20
        ),
        cost_estimate=pl.CostEstimate(
            flops=6 * 2 * 2048 * W * W, bytes_accessed=3 << 20, transcendentals=2048 * W
        ),
    )(tokens.reshape(chunks, m, W), cotangent.reshape(chunks, m, W), weight_in, weight_out)


def hand_over(*refs):
    held, given, rooms, arrived, done = refs[:4], refs[4:8], refs[8:12], refs[12], refs[13]
    ways = []
    for i in range(4):
        rows = held[i].shape[0] // parts_of_result
        for j in range(parts_of_result):
            part = pl.ds(j * rows, rows)
            room = rooms[i].at[part]
            ways.append((
                pltpu.make_async_copy(held[i].at[part], room, arrived.at[i, j]),
                pltpu.make_async_copy(room, given[i].at[part], done.at[i, j]),
            ))
    for come, _ in ways:
        come.start()
    for come, go in ways:
        come.wait()
        go.start()
    for _, go in ways:
        go.wait()


def on_device(tokens, weight_in, weight_out, cotangent):
    output, grad_tokens, grad_in, grad_out = fused(tokens, cotangent, weight_in, weight_out)
    results = (output.reshape(128, W), grad_tokens.reshape(128, W), grad_in, grad_out)
    anywhere = pl.BlockSpec(memory_space=pl.ANY)
    return pl.pallas_call(
        hand_over,
        out_shape=[jax.ShapeDtypeStruct(r.shape, r.dtype) for r in results],
        in_specs=[anywhere] * 4,
        out_specs=[anywhere] * 4,
        scratch_shapes=[pltpu.VMEM(r.shape, r.dtype) for r in results]
        + [pltpu.SemaphoreType.DMA((4, parts_of_result))] * 2,
    )(*results)


def solution(mesh):
    placed = (P("row", "col"),) * 4
    return jax.shard_map(
        on_device, mesh=mesh, in_specs=placed, out_specs=placed, check_vma=False
    )
```
